256 devices in a mesh: dp: 32 (over y, x, core), mp: 8 (over z).
Axes of the slice: x: 4, y: 4, z: 8, core: 2. Of those that a mesh axis runs over, the one named last changes fastest.
Arguments:
- patches: bfloat16 [57344, 3072], P('dp', 'mp'), may hold values from -120 to 120
- labels: int32 [224, 256], P('dp'), may hold values from -1 to 1, as said below
- ln_gain: float32 [3072], replicated, may hold values from 0.5 to 2
- w_qkv: bfloat16 [3, 3072, 3072], P(None, None, 'mp'), may hold values from -0.109375 to 0.109375
- qk_gain: float32 [2, 3072], P(None, 'mp'), may hold values from 0.5 to 2
- w_out: bfloat16 [3072, 3072], P('mp'), may hold values from -0.109375 to 0.109375
Outputs:
- encoded: bfloat16 [57344, 3072], P('dp', 'mp')
The draws below stay inside these ranges and needn't reach their ends.
Inputs may be any that keep to these rules, and one draw needn't show every extreme that they name: Row p of labels is pack p; group g holds packs g * 7 to (g + 1) * 7 - 1. A pack is either all -1 (empty) or holds image numbers that never fall along the pack. A group's non-empty packs come first. Packs 4 and beyond of a group are non-empty only in groups g below 16 whose g mod 4 is one value (which one varies). For every group g, its non-empty packs among its first 4, plus 1 if pack 4 of group (g - 1) mod 32 is non-empty, plus 1 if pack 5 of group (g - 16) mod 32 is non-empty, plus 1 if pack 6 of group (g + 1) mod 32 is non-empty, is at most 4, equal to it for some group; some group has all 7 packs non-empty.
All inputs are finite; a program needn't handle non-finite values.
Results may differ from the reference program's by a relative error of at most 0.019.
Values may be sent and summed in bfloat16 or wider, within the bound.
No kernel may reach another device: no remote copies, remote signals or barrier semaphores. Data moves between devices by JAX's collectives and lax.ppermute only.
A program may use at most 128 MiB of HBM per device.

```python
import math
from functools import partial
import jax
import jax.numpy as jnp
from jax import lax

HEADS = 24
HEAD_DIM = 128
D = 3072
PACK = 256
WORK_P = 4
SURPLUS = 3
HOME_P = 7
ROWS = 57344
N_DP = 32
N_MP = 8


def draw_patches(key, part):
    key = jax.random.fold_in(key, 11)
    key_base, key_column, key_row = jax.random.split(key, 3)
    column_scale = jnp.exp(jax.random.uniform(key_column, (D,), minval=0.0, maxval=math.log(10.0)))
    row_scale = jnp.exp(jax.random.uniform(key_row, (ROWS, 1), minval=math.log(0.3), maxval=math.log(3.0)))
    base_values = jnp.clip(jax.random.normal(key_base, (ROWS, D)), -4.0, 4.0)
    values = base_values * column_scale * row_scale
    return values.astype(jnp.bfloat16)


def draw_labels(key, part):
    key = jax.random.fold_in(key, 5)
    key_phase, key_surplus, key_light, key_heavy, key_cuts, key_enabled = jax.random.split(key, 6)
    group_index = jnp.arange(N_DP)
    phase = jax.random.randint(key_phase, (), 0, 4)
    sender = (group_index % 4 == phase) & (group_index < N_DP // 2)
    surplus = jax.random.randint(key_surplus, (N_DP,), 0, SURPLUS + 1)
    surplus = jnp.where(group_index == phase, SURPLUS, surplus)
    surplus = jnp.where(sender, surplus, 0)
    offset_list = [1, N_DP // 2, N_DP - 1]
    incoming = jnp.zeros((N_DP,), jnp.int32)
    for offset_index in range(SURPLUS):
        offset_value = offset_list[offset_index]
        source_group = (group_index - offset_value) % N_DP
        incoming = incoming + (surplus[source_group] > offset_index).astype(jnp.int32)
    free_room = WORK_P - incoming
    picked = jax.random.randint(key_light, (N_DP,), 0, free_room + 1)
    light_load = jnp.where(group_index == phase + 1, free_room, picked)
    unused_heavy = jax.random.randint(key_heavy, (N_DP,), 0, WORK_P + 1)
    heavy_load = jnp.where(surplus > 0, WORK_P + surplus, unused_heavy)
    group_load = jnp.where(sender, heavy_load, light_load)
    pack_index = jnp.arange(HOME_P)
    alive = pack_index[None, :] < group_load[:, None]
    eighth = PACK // 8
    cut_point = PACK // 2 - eighth + jax.random.randint(key_cuts, (N_DP, HOME_P), 0, 2 * eighth)
    enabled = jax.random.randint(key_enabled, (N_DP, HOME_P), 0, 2)
    forced = (group_index[:, None] == phase) & (pack_index[None, :] == 0)
    enabled = jnp.where(forced, 1, enabled)
    position = jnp.arange(PACK)
    reached = (cut_point[:, :, None] <= position[None, None, :]).astype(jnp.int32)
    image_number = reached * enabled[:, :, None]
    labels = jnp.where(alive[:, :, None], image_number, -1)
    return labels.reshape(N_DP * HOME_P, PACK).astype(jnp.int32)


def shard_levels(rng, shape, cuts, low, largest):
    gain, own = 1.0, jax.random.fold_in(rng, 6)
    for dim, shards_of in cuts:
        steps = jnp.exp(jax.random.uniform(jax.random.fold_in(own, dim), (shards_of,), jnp.float32, low / len(cuts), largest / len(cuts)))
        gain = gain * jnp.repeat(steps, shape[dim] // shards_of).reshape([-1 if axis == dim else 1 for axis in range(len(shape))])
    return gain


def centred(stream_key, dims, scale, most, cuts=(), held_as=jnp.bfloat16):
    level = shard_levels(stream_key, dims, cuts, -0.22, 0.18) if cuts else 1.0
    drawn = jax.random.normal(stream_key, dims, jnp.float32) * scale * level
    return jnp.minimum(jnp.maximum(drawn, -most), most).astype(held_as)


def setup_inputs(seed: int = 0) -> dict:
    splits = jax.random.split(jax.random.key(seed), 7)
    patches = draw_patches(jax.random.fold_in(splits[6], 71), 0)
    labels = draw_labels(jax.random.fold_in(splits[6], 71), 0)
    ln_gain = jnp.clip(jnp.exp(jax.random.uniform(splits[2], (D,), jnp.float32, math.log(0.5), math.log(2.0))), 0.5, 2.0)
    w_qkv = centred(splits[3], (3, D, HEADS * HEAD_DIM), D ** -0.5, 0.109375, ((2, 8),))
    qk_gain = jnp.clip(jnp.exp(math.log(2.0) - 1.3862944 * jax.random.uniform(splits[4], (2, HEADS * HEAD_DIM), jnp.float32) ** shard_levels(splits[4], (2, HEADS * HEAD_DIM), ((1, 8),), -0.2, 0.2)), 0.5, 2.0)
    w_out = centred(splits[5], (HEADS * HEAD_DIM, D), (HEADS * HEAD_DIM) ** -0.5, 0.109375, ((0, 8),))
    return {"patches": patches, "labels": labels, "ln_gain": ln_gain, "w_qkv": w_qkv, "qk_gain": qk_gain, "w_out": w_out}


EPSILON = 1e-06

def layer_norm(values, norm_gain):
    row_mean = lax.optimization_barrier(jnp.mean(values, axis=-1, keepdims=True))
    centered = values - row_mean
    spread = lax.optimization_barrier(jnp.mean(centered * centered, axis=-1, keepdims=True))
    return centered * lax.rsqrt(spread + EPSILON) * norm_gain

def encode_group(operands, ln_gain, w_qkv, qk_gain, w_out):
    group_rows, packed = operands
    row_count = group_rows.shape[0]
    pack_count = row_count // PACK
    normed = layer_norm(group_rows.astype(jnp.float32), ln_gain).astype(jnp.bfloat16)
    query_raw = jnp.dot(normed, w_qkv[0], preferred_element_type=jnp.float32)
    key_raw = jnp.dot(normed, w_qkv[1], preferred_element_type=jnp.float32)
    value_raw = jnp.dot(normed, w_qkv[2], preferred_element_type=jnp.float32)
    heads_gain = qk_gain.reshape(2, HEADS, HEAD_DIM)
    queries = layer_norm(query_raw.reshape(row_count, HEADS, HEAD_DIM), heads_gain[0]).astype(jnp.bfloat16)
    key_heads = layer_norm(key_raw.reshape(row_count, HEADS, HEAD_DIM), heads_gain[1]).astype(jnp.bfloat16)
    values = value_raw.astype(jnp.bfloat16)
    query_packs = queries.reshape(pack_count, PACK, HEADS, HEAD_DIM).astype(jnp.float32)
    key_packs = key_heads.reshape(pack_count, PACK, HEADS, HEAD_DIM).astype(jnp.float32)
    value_packs = values.reshape(pack_count, PACK, HEADS, HEAD_DIM).astype(jnp.float32)
    scores = jnp.einsum('pqhe,pkhe->phqk', query_packs, key_packs) * HEAD_DIM ** (-0.5)
    allowed = packed[:, None, :, None] == packed[:, None, None, :]
    exponent = jnp.where(allowed, jnp.exp(scores), 0.0)
    weights = (exponent / lax.optimization_barrier(jnp.sum(exponent, axis=-1, keepdims=True))).astype(jnp.bfloat16)
    attended = jnp.einsum('phqk,pkhe->pqhe', weights.astype(jnp.float32), value_packs)
    attended = attended.astype(jnp.bfloat16).reshape(row_count, HEADS * HEAD_DIM)
    grouped = attended.reshape(row_count, N_MP, -1).astype(jnp.float32)
    out_grouped = w_out.reshape(N_MP, -1, D).astype(jnp.float32)
    partials = jnp.einsum('rmc,mcd->mrd', grouped, out_grouped)
    rounded = lax.optimization_barrier(partials.astype(jnp.bfloat16))
    summed = lax.optimization_barrier(jnp.sum(rounded.astype(jnp.float32), axis=0))
    alive = jnp.repeat(packed[:, 0] >= 0, PACK)
    return jnp.where(alive[:, None], summed, 0.0).astype(jnp.bfloat16)

def reference(patches, labels, ln_gain, w_qkv, qk_gain, w_out):
    group_rows = patches.reshape(N_DP, -1, D)
    packed = labels.reshape(N_DP, -1, PACK)
    encoder = partial(encode_group, ln_gain=ln_gain, w_qkv=w_qkv, qk_gain=qk_gain, w_out=w_out)
    encoded = lax.map(encoder, (group_rows, packed))
    return encoded.reshape(-1, D)
```

```python
import functools

import jax
import jax.numpy as jnp
from jax import lax
from jax.experimental import pallas as pl
from jax.experimental.pallas import tpu as pltpu
from jax.sharding import PartitionSpec as P

HEAD_DIM = 128
WORK_P = 4
EPSILON = 1e-06
MESH_MP = 8
VMEM_LIMIT = 30 * 1024 * 1024


def normalize(values, norm_gain):
    row_mean = jnp.mean(values, axis=-1, keepdims=True)
    centered = values - row_mean
    spread = jnp.mean(centered * centered, axis=-1, keepdims=True)
    return centered * lax.rsqrt(spread + EPSILON) * norm_gain


def encode_kernel(n_mp, slot, slots, me_ref, lab_ref, gain_ref, qk_ref, *refs):
    blocks, refs = refs[:9], refs[9:]
    wqkv_hbm, wout_hbm, o0, ou1, od1, ou2, od2, ou3, od3, o4, normed, wqkv, wout, sems = refs
    copies = [
        pltpu.make_async_copy(wqkv_hbm.at[t], wqkv.at[t], sems.at[t]) for t in range(3)
    ]
    copies.append(pltpu.make_async_copy(wout_hbm, wout, sems.at[3]))
    for copy in copies:
        copy.start()
    me = me_ref[0]
    rows, width = o0.shape
    features = n_mp * width
    half = rows // 2
    mine = pl.ds(slot * rows, rows)
    pieces = [
        (ref.at[mine], offset, 0, rows)
        for ref, offset in zip(blocks[:7], (0, -1, 1, -2, 2, -3, 3))
    ]
    if slots == 1:
        pieces += [(blocks[7], 4, 0, half), (blocks[8], 4, half, half)]
    else:
        pieces.append((blocks[7 + slot], 4, 0, rows))

    def columns(offset):
        return pl.ds(pl.multiple_of(lax.rem(me + offset + n_mp, n_mp) * width, width), width)

    def reduced(function):
        total = jnp.zeros((rows, 128), jnp.float32)
        split = []
        for ref, _, start, size in pieces:
            part = function(ref[...].astype(jnp.float32), start, size)
            part = sum(part[:, c:c + 128] for c in range(0, width, 128))
            if size == rows:
                total = total + part
            else:
                split.append(part)
        if split:
            total = total + jnp.concatenate(split, axis=0)
        return jnp.sum(total, axis=1, keepdims=True) * (1.0 / features)

    def squared(part, start, size):
        part = part - mean[start:start + size]
        return part * part

    mean = reduced(lambda part, start, size: part)
    scale = lax.rsqrt(reduced(squared) + EPSILON)
    for ref, offset, start, size in pieces:
        cols = columns(offset)
        part = (ref[...].astype(jnp.float32) - mean[start:start + size]) * scale[start:start + size]
        normed[start:start + size, cols] = (part * gain_ref[0:1, cols]).astype(jnp.bfloat16)

    projected = []
    for t in range(3):
        copies[t].wait()
        projected.append(
            jnp.dot(normed[...], wqkv[t], preferred_element_type=jnp.float32)
        )
    label_row = jnp.broadcast_to(lab_ref[...].astype(jnp.float32), (rows, rows))
    allowed = label_row == label_row.T
    attended = []
    for h in range(width // HEAD_DIM):
        cut = slice(h * HEAD_DIM, (h + 1) * HEAD_DIM)
        query = normalize(projected[0][:, cut], qk_ref[0:1, cut]).astype(jnp.bfloat16)
        key = normalize(projected[1][:, cut], qk_ref[1:2, cut]).astype(jnp.bfloat16)
        value = projected[2][:, cut].astype(jnp.bfloat16)
        score = lax.dot_general(
            query, key, (((1,), (1,)), ((), ())), preferred_element_type=jnp.float32
        ) * HEAD_DIM ** (-0.5)
        exponent = jnp.where(allowed, jnp.exp(score), 0.0)
        weight = exponent * (1.0 / jnp.sum(exponent, axis=1, keepdims=True))
        attended.append(
            jnp.dot(weight.astype(jnp.bfloat16), value, preferred_element_type=jnp.float32)
            .astype(jnp.bfloat16)
        )
    attended = jnp.concatenate(attended, axis=1)
    copies[3].wait()
    for ref, offset in ((o4, 4), (ou3, 3), (od3, -3), (ou2, 2), (od2, -2), (ou1, 1), (od1, -1), (o0, 0)):
        ref[...] = jnp.dot(
            attended, wout[:, columns(offset)], preferred_element_type=jnp.float32
        ).astype(jnp.bfloat16)


def encode(me, labels, gain, qk_gain, blocks, slot, slots, w_qkv, w_out):
    n_mp = MESH_MP
    rows, width = blocks[0].shape[0] // slots, blocks[0].shape[1]
    features = n_mp * width
    vmem = pl.BlockSpec(memory_space=pltpu.VMEM)
    hbm = pl.BlockSpec(memory_space=pl.ANY)
    flops = 2 * rows * features * 3 * width + 2 * rows * width * features + 4 * rows * rows * width
    return pl.pallas_call(
        functools.partial(encode_kernel, n_mp, slot, slots),
        out_shape=[jax.ShapeDtypeStruct((rows, width), jnp.bfloat16)] * 8,
        in_specs=[pl.BlockSpec(memory_space=pltpu.SMEM)] + [vmem] * 12 + [hbm] * 2,
        out_specs=[vmem] * 8,
        scratch_shapes=[
            pltpu.VMEM((rows, features), jnp.bfloat16),
            pltpu.VMEM(w_qkv.shape, jnp.bfloat16),
            pltpu.VMEM(w_out.shape, jnp.bfloat16),
            pltpu.SemaphoreType.DMA((4,)),
        ],
        compiler_params=pltpu.CompilerParams(vmem_limit_bytes=VMEM_LIMIT),
        cost_estimate=pl.CostEstimate(
            flops=flops,
            bytes_accessed=2 * (w_qkv.size + w_out.size) + 4 * rows * features,
            transcendentals=rows * rows * width // HEAD_DIM,
        ),
    )(me, labels, gain, qk_gain, *blocks, w_qkv, w_out)


def pack_kernel(kept, labels_smem, labels_ref, patches_hbm, *refs):
    outs, sems = refs[:-1], refs[-1]
    pack_rows = labels_ref.shape[1]
    copies = []
    for k, out in enumerate(outs):
        rows = pl.ds((kept + k) * pack_rows, pack_rows)
        copies.append(
            pltpu.make_async_copy(patches_hbm.at[rows], out.at[pl.ds(0, pack_rows)], sems.at[k])
        )
        copies[-1].start()
    for k, out in enumerate(outs):
        tail = out.shape[0] - pack_rows
        tags = labels_ref[kept + k:kept + k + 1].astype(jnp.float32) + 1.0
        tags = jnp.broadcast_to(tags, (tail, pack_rows)).astype(jnp.bfloat16)
        out[pack_rows:, :pack_rows] = tags
        out[pack_rows:, pack_rows:] = jnp.zeros((tail, out.shape[1] - pack_rows), jnp.bfloat16)
        copies[k].wait()

        @pl.when(labels_smem[kept + k, 0] < 0)
        def _(out=out):
            out[:pack_rows] = jnp.zeros((pack_rows, out.shape[1]), jnp.bfloat16)


def pack_spare(labels, patches, kept, spare):
    pack_rows, width = labels.shape[1], patches.shape[1]
    vmem = pl.BlockSpec(memory_space=pltpu.VMEM)
    return pl.pallas_call(
        functools.partial(pack_kernel, kept),
        out_shape=[jax.ShapeDtypeStruct((pack_rows + 16, width), jnp.bfloat16)] * spare,
        in_specs=[pl.BlockSpec(memory_space=pltpu.SMEM), vmem, pl.BlockSpec(memory_space=pl.ANY)],
        out_specs=[vmem] * spare,
        scratch_shapes=[pltpu.SemaphoreType.DMA((spare,))],
        cost_estimate=pl.CostEstimate(
            flops=0, bytes_accessed=4 * spare * pack_rows * width, transcendentals=0
        ),
    )(labels, labels, patches)


def merge_kernel(last, labels_smem, labels_ref, patches_hbm, a0, a1, a2, rows_ref, tags_ref, sem):
    pack_rows = labels_ref.shape[1]
    own = labels_smem[last, 0] >= 0

    @pl.when(own)
    def _():
        source = patches_hbm.at[pl.ds(last * pack_rows, pack_rows)]
        copy = pltpu.make_async_copy(source, rows_ref, sem)
        copy.start()
        copy.wait()
        tags_ref[...] = labels_ref[last:last + 1]

    @pl.when(jnp.logical_not(own))
    def _():
        rows_ref[...] = a0[:pack_rows] + a1[:pack_rows] + a2[:pack_rows]
        tags = a0[pack_rows:, :pack_rows] + a1[pack_rows:, :pack_rows] + a2[pack_rows:, :pack_rows]
        tags_ref[...] = tags.astype(jnp.float32)[0:1].astype(jnp.int32) - 1


def merge_last(labels, patches, arrived, last):
    pack_rows, width = labels.shape[1], patches.shape[1]
    vmem = pl.BlockSpec(memory_space=pltpu.VMEM)
    return pl.pallas_call(
        functools.partial(merge_kernel, last),
        out_shape=[
            jax.ShapeDtypeStruct((pack_rows, width), jnp.bfloat16),
            jax.ShapeDtypeStruct((1, pack_rows), jnp.int32),
        ],
        in_specs=[pl.BlockSpec(memory_space=pltpu.SMEM), vmem, pl.BlockSpec(memory_space=pl.ANY)]
        + [vmem] * 3,
        out_specs=[vmem] * 2,
        scratch_shapes=[pltpu.SemaphoreType.DMA(())],
        cost_estimate=pl.CostEstimate(
            flops=0, bytes_accessed=8 * pack_rows * width, transcendentals=0
        ),
    )(labels, labels, patches, *arrived)


def finish_kernel(labels_smem, s0, own, rising, falling, s3, r0, r1, r2, out_ref):
    rows = s0.shape[0]

    def put(pack, values):
        live = labels_smem[pack, 0] >= 0
        out_ref[pack * rows:(pack + 1) * rows] = jnp.where(live, values, 0.0).astype(jnp.bfloat16)

    put(0, s0[...].astype(jnp.float32))
    for k in range(2):
        cut = pl.ds(k * rows, rows)
        put(1 + k, own[cut].astype(jnp.float32) + rising[cut].astype(jnp.float32)
            + falling[cut].astype(jnp.float32))
    for k, ref in enumerate((s3, r0, r1, r2)):
        put(3 + k, ref[...].astype(jnp.float32))


def finish(labels, *parts):
    home_packs, pack_rows = labels.shape
    width = parts[0].shape[1]
    vmem = pl.BlockSpec(memory_space=pltpu.VMEM)
    return pl.pallas_call(
        finish_kernel,
        out_shape=jax.ShapeDtypeStruct((home_packs * pack_rows, width), jnp.bfloat16),
        in_specs=[pl.BlockSpec(memory_space=pltpu.SMEM)] + [vmem] * len(parts),
        out_specs=vmem,
        cost_estimate=pl.CostEstimate(
            flops=0, bytes_accessed=4 * home_packs * pack_rows * width, transcendentals=0
        ),
    )(labels, *parts)


def after(value, *others):
    return lax.optimization_barrier((value,) + others)[0]


def gather_chain(block, up, down, hold=()):
    half = block.shape[0] // 2
    got = [block]
    rising = falling = after(block, *hold) if hold else block
    for _ in range(3):
        rising = lax.ppermute(rising, "mp", up)
        falling = lax.ppermute(falling, "mp", down)
        got += [rising, falling]
    got.append(lax.ppermute(rising[:half], "mp", up))
    got.append(lax.ppermute(falling[half:], "mp", down))
    return got


def add(first, second):
    return (first.astype(jnp.float32) + second.astype(jnp.float32)).astype(jnp.bfloat16)


def scatter_chain(partials, up, down, hold=()):
    o0, u1, d1, u2, d2, u3, d3, o4 = partials
    half = o0.shape[0] // 2
    if hold:
        o4 = after(o4, *hold)
    rising = lax.ppermute(o4[:half], "mp", up)
    falling = lax.ppermute(o4[half:], "mp", down)
    rising = jnp.concatenate([add(u3[:half], rising), u3[half:]], axis=0)
    falling = jnp.concatenate([d3[:half], add(d3[half:], falling)], axis=0)
    rising = lax.ppermute(rising, "mp", up)
    falling = lax.ppermute(falling, "mp", down)
    rising = lax.ppermute(add(u2, rising), "mp", up)
    falling = lax.ppermute(add(d2, falling), "mp", down)
    rising = lax.ppermute(add(u1, rising), "mp", up)
    falling = lax.ppermute(add(d1, falling), "mp", down)
    return o0, rising, falling


def total(parts):
    return sum(part.astype(jnp.float32) for part in parts).astype(jnp.bfloat16)


def local(patches, labels, ln_gain, w_qkv, qk_gain, w_out):
    groups = lax.axis_size("dp")
    n_mp = lax.axis_size("mp")
    up = [(i, (i + 1) % n_mp) for i in range(n_mp)]
    down = [(i, (i - 1) % n_mp) for i in range(n_mp)]
    home_packs, pack_rows = labels.shape
    spare = home_packs - WORK_P
    last = WORK_P - 1
    offsets = [1, groups // 2, groups - 1][:spare]
    me = lax.axis_index("mp").astype(jnp.int32).reshape(1)
    gain = ln_gain.reshape(1, -1)

    def run(got, tags, slot, slots):
        return encode(me, tags.reshape(1, -1), gain, qk_gain, got, slot, slots, w_qkv, w_out)

    first = gather_chain(patches[:pack_rows], up, down)
    middle = gather_chain(patches[pack_rows:last * pack_rows], up, down)

    sent = pack_spare(labels, patches, WORK_P, spare)
    arrived = [
        lax.ppermute(sent[k], "dp", [(i, (i + offset) % groups) for i in range(groups)])
        for k, offset in enumerate(offsets)
    ]
    last_rows, last_labels = merge_last(labels, patches, arrived, last)
    final = gather_chain(last_rows, up, down)

    sum_first = total(scatter_chain(run(first, labels[0], 0, 1), up, down))
    sum_last = total(scatter_chain(run(final, last_labels, 0, 1), up, down))
    returned = [
        lax.ppermute(sum_last, "dp", [(i, (i - offset) % groups) for i in range(groups)])
        for offset in offsets
    ]
    parts = [run(middle, labels[1 + k], k, 2) for k in range(2)]
    joined = [jnp.concatenate(pair, axis=0) for pair in zip(*parts)]
    own, rising, falling = scatter_chain(joined, up, down)
    return finish(labels, sum_first, own, rising, falling, sum_last, *returned)


def solution(mesh):
    placed = (P("dp", "mp"), P("dp", None), P(), P(None, None, "mp"), P(None, "mp"), P("mp", None))
    return jax.shard_map(
        local, mesh=mesh, in_specs=placed, out_specs=P("dp", "mp"), check_vma=False
    )
```

```python
import functools

import jax
import jax.numpy as jnp
from jax import lax
from jax.experimental import pallas as pl
from jax.experimental.pallas import tpu as pltpu
from jax.sharding import PartitionSpec as P

HEAD_DIM = 128
WORK_P = 4
EPSILON = 1e-06
MESH_MP = 8
VMEM_LIMIT = 52 * 1024 * 1024
SMALL_VMEM = 8 * 1024 * 1024


def normalize(values, norm_gain):
    row_mean = jnp.mean(values, axis=-1, keepdims=True)
    centered = values - row_mean
    spread = jnp.mean(centered * centered, axis=-1, keepdims=True)
    return centered * lax.rsqrt(spread + EPSILON) * norm_gain


def encode_kernel(n_mp, slot, row, me_ref, lab_ref, gain_ref, qk_ref, *refs):
    blocks, refs = refs[:9], refs[9:]
    wqkv_hbm, wout_hbm, o0, ou1, od1, ou2, od2, ou3, od3, o4, held, normed, wqkv, wout, sems = refs
    rows, width = o0.shape
    features = n_mp * width
    mine = pl.ds(slot * rows, rows)
    sources = [ref.at[mine] for ref in blocks[:7]] + [blocks[7 + slot]]
    fetches = [
        pltpu.make_async_copy(source, held.at[k], sems.at[k]) for k, source in enumerate(sources)
    ]
    loads = [
        pltpu.make_async_copy(wqkv_hbm.at[t], wqkv.at[t], sems.at[8 + t]) for t in range(3)
    ] + [pltpu.make_async_copy(wout_hbm, wout, sems.at[11])]
    for copy in fetches + loads:
        copy.start()
    me = me_ref[0]

    def columns(offset):
        return pl.ds(pl.multiple_of(lax.rem(me + offset + n_mp, n_mp) * width, width), width)

    pieces = [(held.at[k], columns(o)) for k, o in enumerate((0, -1, 1, -2, 2, -3, 3, 4))]

    def folded(part):
        return sum(part[:, c:c + 128] for c in range(0, width, 128))

    sums = jnp.zeros((rows, 128), jnp.float32)
    for (ref, _), copy in zip(pieces, fetches):
        copy.wait()
        sums = sums + folded(ref[...].astype(jnp.float32))
    mean = jnp.sum(sums, axis=1, keepdims=True) * (1.0 / features)
    sums = jnp.zeros((rows, 128), jnp.float32)
    for ref, _ in pieces:
        part = ref[...].astype(jnp.float32) - mean
        sums = sums + folded(part * part)
    spread = jnp.sum(sums, axis=1, keepdims=True) * (1.0 / features)
    scale = lax.rsqrt(spread + EPSILON)
    for ref, cols in pieces:
        part = (ref[...].astype(jnp.float32) - mean) * scale
        normed[:, cols] = (part * gain_ref[0:1, cols]).astype(jnp.bfloat16)

    projected = []
    for t in range(3):
        loads[t].wait()
        projected.append(jnp.dot(normed[...], wqkv[t], preferred_element_type=jnp.float32))
    label_row = jnp.broadcast_to(lab_ref[row:row + 1].astype(jnp.float32), (rows, rows))
    allowed = label_row == label_row.T
    attended = []
    for h in range(width // HEAD_DIM):
        cut = slice(h * HEAD_DIM, (h + 1) * HEAD_DIM)
        query = normalize(projected[0][:, cut], qk_ref[0:1, cut]).astype(jnp.bfloat16)
        key = normalize(projected[1][:, cut], qk_ref[1:2, cut]).astype(jnp.bfloat16)
        value = projected[2][:, cut].astype(jnp.bfloat16)
        score = lax.dot_general(
            query, key, (((1,), (1,)), ((), ())), preferred_element_type=jnp.float32
        ) * HEAD_DIM ** (-0.5)
        exponent = jnp.where(allowed, jnp.exp(score), 0.0)
        weight = exponent * (1.0 / jnp.sum(exponent, axis=1, keepdims=True))
        attended.append(
            jnp.dot(weight.astype(jnp.bfloat16), value, preferred_element_type=jnp.float32)
            .astype(jnp.bfloat16)
        )
    attended = jnp.concatenate(attended, axis=1)
    loads[3].wait()
    for ref, offset in ((o4, 4), (ou3, 3), (od3, -3), (ou2, 2), (od2, -2), (ou1, 1), (od1, -1), (o0, 0)):
        ref[...] = jnp.dot(
            attended, wout[:, columns(offset)], preferred_element_type=jnp.float32
        ).astype(jnp.bfloat16)


def encode(me, labels, row, gain, qk_gain, blocks, slot, w_qkv, w_out):
    n_mp = MESH_MP
    rows, width = blocks[0].shape[0] // 2, blocks[0].shape[1]
    features = n_mp * width
    vmem = pl.BlockSpec(memory_space=pltpu.VMEM)
    hbm = pl.BlockSpec(memory_space=pltpu.HBM)
    return pl.pallas_call(
        functools.partial(encode_kernel, n_mp, slot, row),
        out_shape=[jax.ShapeDtypeStruct((rows, width), jnp.bfloat16)] * 8,
        in_specs=[pl.BlockSpec(memory_space=pltpu.SMEM)] + [vmem] * 3 + [hbm] * 11,
        out_specs=[vmem] * 8,
        scratch_shapes=[
            pltpu.VMEM((n_mp, rows, width), jnp.bfloat16),
            pltpu.VMEM((rows, features), jnp.bfloat16),
            pltpu.VMEM(w_qkv.shape, jnp.bfloat16),
            pltpu.VMEM(w_out.shape, jnp.bfloat16),
            pltpu.SemaphoreType.DMA((12,)),
        ],
        compiler_params=pltpu.CompilerParams(vmem_limit_bytes=VMEM_LIMIT),
        cost_estimate=pl.CostEstimate(
            flops=2 * rows * features * 4 * width,
            bytes_accessed=4 * rows * features,
            transcendentals=0,
        ),
    )(me, labels, gain, qk_gain, *blocks, w_qkv, w_out)


def pack_kernel(kept, labels_smem, labels_ref, patches_hbm, *refs):
    outs, sems = refs[:-1], refs[-1]
    pack_rows = labels_ref.shape[1]
    copies = []
    for k, out in enumerate(outs):
        rows = pl.ds((kept + k) * pack_rows, pack_rows)
        copies.append(
            pltpu.make_async_copy(patches_hbm.at[rows], out.at[pl.ds(0, pack_rows)], sems.at[k])
        )
        copies[-1].start()
    for k, out in enumerate(outs):
        tail = out.shape[0] - pack_rows
        tags = labels_ref[kept + k:kept + k + 1].astype(jnp.float32) + 1.0
        tags = jnp.broadcast_to(tags, (tail, pack_rows)).astype(jnp.bfloat16)
        out[pack_rows:, :pack_rows] = tags
        out[pack_rows:, pack_rows:] = jnp.zeros((tail, out.shape[1] - pack_rows), jnp.bfloat16)
        copies[k].wait()

        @pl.when(labels_smem[kept + k, 0] < 0)
        def _(out=out):
            out[:pack_rows] = jnp.zeros((pack_rows, out.shape[1]), jnp.bfloat16)


def pack_spare(labels, patches, kept, spare):
    pack_rows, width = labels.shape[1], patches.shape[1]
    vmem = pl.BlockSpec(memory_space=pltpu.VMEM)
    return pl.pallas_call(
        functools.partial(pack_kernel, kept),
        out_shape=[jax.ShapeDtypeStruct((pack_rows + 16, width), jnp.bfloat16)] * spare,
        in_specs=[pl.BlockSpec(memory_space=pltpu.SMEM), vmem, pl.BlockSpec(memory_space=pltpu.HBM)],
        out_specs=[vmem] * spare,
        scratch_shapes=[pltpu.SemaphoreType.DMA((spare,))],
        compiler_params=pltpu.CompilerParams(vmem_limit_bytes=SMALL_VMEM),
        cost_estimate=pl.CostEstimate(
            flops=0, bytes_accessed=4 * spare * pack_rows * width, transcendentals=0
        ),
    )(labels, labels, patches)


def merge_kernel(last, labels_smem, labels_ref, patches_hbm, a0, a1, a2, rows_ref, tags_ref, sems):
    pack_rows = labels_ref.shape[1]
    own = labels_smem[last, 0] >= 0
    head = pltpu.make_async_copy(
        patches_hbm.at[pl.ds(0, pack_rows)], rows_ref.at[pl.ds(0, pack_rows)], sems.at[0]
    )
    head.start()

    @pl.when(own)
    def _():
        source = patches_hbm.at[pl.ds(last * pack_rows, pack_rows)]
        copy = pltpu.make_async_copy(source, rows_ref.at[pl.ds(pack_rows, pack_rows)], sems.at[1])
        copy.start()
        copy.wait()
        tags_ref[...] = labels_ref[last:last + 1]

    @pl.when(jnp.logical_not(own))
    def _():
        rows_ref[pack_rows:] = a0[:pack_rows] + a1[:pack_rows] + a2[:pack_rows]
        tags = a0[pack_rows:, :pack_rows] + a1[pack_rows:, :pack_rows] + a2[pack_rows:, :pack_rows]
        tags_ref[...] = tags.astype(jnp.float32)[0:1].astype(jnp.int32) - 1

    head.wait()


def merge_last(labels, patches, arrived, last):
    pack_rows, width = labels.shape[1], patches.shape[1]
    vmem = pl.BlockSpec(memory_space=pltpu.VMEM)
    return pl.pallas_call(
        functools.partial(merge_kernel, last),
        out_shape=[
            jax.ShapeDtypeStruct((2 * pack_rows, width), jnp.bfloat16),
            jax.ShapeDtypeStruct((1, pack_rows), jnp.int32),
        ],
        in_specs=[pl.BlockSpec(memory_space=pltpu.SMEM), vmem, pl.BlockSpec(memory_space=pltpu.HBM)]
        + [vmem] * 3,
        out_specs=[vmem] * 2,
        scratch_shapes=[pltpu.SemaphoreType.DMA((2,))],
        compiler_params=pltpu.CompilerParams(vmem_limit_bytes=SMALL_VMEM),
        cost_estimate=pl.CostEstimate(
            flops=0, bytes_accessed=8 * pack_rows * width, transcendentals=0
        ),
    )(labels, labels, patches, *arrived)


def finish_kernel(labels_smem, x1, x2, rising, falling, first, last, r0, r1, r2, out_ref):
    rows = first.shape[0]
    terms = [[first]]
    for k, own in enumerate((x1, x2)):
        cut = pl.ds(k * rows, rows)
        terms.append([own, rising.at[cut], falling.at[cut]])
    terms += [[last], [r0], [r1], [r2]]
    for pack, parts in enumerate(terms):
        values = sum(part[...].astype(jnp.float32) for part in parts)
        live = labels_smem[pack, 0] >= 0
        out_ref[pack * rows:(pack + 1) * rows] = jnp.where(live, values, 0.0).astype(jnp.bfloat16)


def finish(labels, *parts):
    home_packs, pack_rows = labels.shape
    width = parts[0].shape[1]
    vmem = pl.BlockSpec(memory_space=pltpu.VMEM)
    return pl.pallas_call(
        finish_kernel,
        out_shape=jax.ShapeDtypeStruct((home_packs * pack_rows, width), jnp.bfloat16),
        in_specs=[pl.BlockSpec(memory_space=pltpu.SMEM)] + [vmem] * len(parts),
        out_specs=vmem,
        compiler_params=pltpu.CompilerParams(vmem_limit_bytes=SMALL_VMEM),
        cost_estimate=pl.CostEstimate(
            flops=0, bytes_accessed=4 * home_packs * pack_rows * width, transcendentals=0
        ),
    )(labels, *parts)


class Order:
    def __init__(self, token):
        self.token = token

    def tie(self, *values):
        tied = lax.optimization_barrier(values + (self.token,))[:-1]
        return tied if len(tied) > 1 else tied[0]

    def mark(self, *values):
        self.token = lax.optimization_barrier((self.token,) + values)[0]


class Ring:
    def __init__(self, order):
        size = lax.axis_size("mp")
        self.order = order
        self.up = [(i, (i + 1) % size) for i in range(size)]
        self.down = [(i, (i - 1) % size) for i in range(size)]

    def send(self, rising, falling):
        rising, falling = self.order.tie(rising, falling)
        self.rising = lax.ppermute(rising, "mp", self.up)
        self.falling = lax.ppermute(falling, "mp", self.down)

    def done(self):
        self.order.mark(self.rising, self.falling)


class Gather(Ring):
    def __init__(self, order, block):
        super().__init__(order)
        self.half = block.shape[0] // 2
        self.blocks = [block]
        self.rising = self.falling = block

    def start(self):
        if len(self.blocks) < 7:
            self.send(self.rising, self.falling)
        else:
            self.send(self.rising[:self.half], self.falling[self.half:])

    def done(self):
        super().done()
        self.blocks += [self.rising, self.falling]


def add(first, second):
    return (first.astype(jnp.float32) + second.astype(jnp.float32)).astype(jnp.bfloat16)


def stack(first, second):
    return jnp.concatenate([first, second], axis=0)


def stack(first, second):
    return jnp.concatenate([first, second], axis=0)


class Scatter(Ring):
    def __init__(self, order, first, second):
        super().__init__(order)
        self.first, self.second = first, second
        self.rows = first[0].shape[0]
        self.step = 0

    def sums(self, at, cut):
        pack = self.first if cut == 0 else self.second
        rows = slice(cut * self.rows, (cut + 1) * self.rows)
        return add(pack[at], self.rising[rows]), add(pack[at + 1], self.falling[rows])

    def start(self):
        one, two = self.first, self.second
        if self.step == 0:
            self.send(one[7], two[7])
        elif self.step == 1:
            self.send(stack(add(one[5], self.rising), two[5]), stack(one[6], add(two[6], self.falling)))
        else:
            (up1, down1), (up2, down2) = (self.sums(7 - 2 * self.step, cut) for cut in range(2))
            self.send(stack(up1, up2), stack(down1, down2))
        self.step += 1

    def last(self, cut):
        end = Ring(self.order)
        end.send(*self.sums(1, cut))
        end.own = (self.first, self.second)[cut][0]
        return end


def total(ring):
    terms = (ring.own, ring.rising, ring.falling)
    return sum(term.astype(jnp.float32) for term in terms).astype(jnp.bfloat16)


def local(patches, labels, ln_gain, w_qkv, qk_gain, w_out):
    groups = lax.axis_size("dp")
    home_packs, pack_rows = labels.shape
    spare = home_packs - WORK_P
    last = WORK_P - 1
    offsets = [1, groups // 2, groups - 1][:spare]
    me = lax.axis_index("mp").astype(jnp.int32).reshape(1)
    gain = ln_gain.reshape(1, -1)
    order = Order(labels[0, :1])

    def over_groups(values, sign):
        return [
            lax.ppermute(value, "dp", [(i, (i + sign * offset) % groups) for i in range(groups)])
            for value, offset in zip(order.tie(*values), offsets)
        ]

    def run(got, tags, row, slot):
        sums = encode(me, tags, row, gain, qk_gain, order.tie(*got.blocks), slot, w_qkv, w_out)
        order.mark(*sums)
        return sums

    def step(ring):
        ring.done()
        ring.start()

    x = Gather(order, patches[pack_rows:last * pack_rows])
    x.start()
    arrived = over_groups(pack_spare(labels, patches, WORK_P, spare), 1)
    step(x)
    order.mark(*arrived)
    rows, last_labels = merge_last(labels, patches, arrived, last)
    y = Gather(order, rows)
    y.start()
    step(x)
    step(y)
    step(x)
    y.done()
    x.done()
    y.start()
    sums1 = run(x, labels, 1, 0)
    step(y)
    sums2 = run(x, labels, 2, 1)
    y.done()
    rx = Scatter(order, sums1, sums2)
    rx.start()
    sums0 = run(y, labels, 0, 0)
    step(rx)
    sums3 = run(y, last_labels, 0, 1)
    step(rx)
    ry = Scatter(order, sums0, sums3)
    ry.start()
    step(ry)
    rx.done()
    step(ry)
    rx.start()
    ry.done()
    end3 = ry.last(1)
    rx.done()
    end0 = ry.last(0)
    end3.done()
    sum3 = total(end3)
    returned = over_groups([sum3] * spare, -1)
    end0.done()
    return finish(
        labels, sums1[0], sums2[0], rx.rising, rx.falling, total(end0), sum3, *returned
    )


def solution(mesh):
    placed = (P("dp", "mp"), P("dp", None), P(), P(None, None, "mp"), P(None, "mp"), P("mp", None))
    return jax.shard_map(
        local, mesh=mesh, in_specs=placed, out_specs=P("dp", "mp"), check_vma=False
    )
```

```python
import functools

import jax
import jax.numpy as jnp
from jax import lax
from jax.experimental import pallas as pl
from jax.experimental.pallas import tpu as pltpu
from jax.sharding import PartitionSpec as P

HEAD_DIM = 128
WORK_P = 4
EPSILON = 1e-06
MESH_MP = 8
VMEM_LIMIT = 52 * 1024 * 1024
SMALL_VMEM = 8 * 1024 * 1024


def normalize(values, norm_gain):
    row_mean = jnp.mean(values, axis=-1, keepdims=True)
    centered = values - row_mean
    spread = jnp.mean(centered * centered, axis=-1, keepdims=True)
    return centered * lax.rsqrt(spread + EPSILON) * norm_gain


def encode_kernel(n_mp, slot, row, me_ref, lab_ref, gain_ref, qk_ref, *refs):
    blocks, refs = refs[:9], refs[9:]
    wqkv_hbm, wout_hbm, o0, ou1, od1, ou2, od2, ou3, od3, o4, held, normed, wqkv, wout, sems = refs
    rows, width = o0.shape
    features = n_mp * width
    mine = pl.ds(slot * rows, rows)
    sources = [ref.at[mine] for ref in blocks[:7]] + [blocks[7 + slot]]
    fetches = [
        pltpu.make_async_copy(source, held.at[k], sems.at[k]) for k, source in enumerate(sources)
    ]
    loads = [
        pltpu.make_async_copy(wqkv_hbm.at[t], wqkv.at[t], sems.at[8 + t]) for t in range(3)
    ] + [pltpu.make_async_copy(wout_hbm, wout, sems.at[11])]
    for copy in fetches + loads:
        copy.start()
    me = me_ref[0]

    def columns(offset):
        return pl.ds(pl.multiple_of(lax.rem(me + offset + n_mp, n_mp) * width, width), width)

    pieces = [(held.at[k], columns(o)) for k, o in enumerate((0, -1, 1, -2, 2, -3, 3, 4))]

    def folded(part):
        return sum(part[:, c:c + 128] for c in range(0, width, 128))

    sums = jnp.zeros((rows, 128), jnp.float32)
    for (ref, _), copy in zip(pieces, fetches):
        copy.wait()
        sums = sums + folded(ref[...].astype(jnp.float32))
    mean = jnp.sum(sums, axis=1, keepdims=True) * (1.0 / features)
    sums = jnp.zeros((rows, 128), jnp.float32)
    for ref, _ in pieces:
        part = ref[...].astype(jnp.float32) - mean
        sums = sums + folded(part * part)
    spread = jnp.sum(sums, axis=1, keepdims=True) * (1.0 / features)
    scale = lax.rsqrt(spread + EPSILON)
    for ref, cols in pieces:
        part = (ref[...].astype(jnp.float32) - mean) * scale
        normed[:, cols] = (part * gain_ref[0:1, cols]).astype(jnp.bfloat16)

    projected = []
    for t in range(3):
        loads[t].wait()
        projected.append(jnp.dot(normed[...], wqkv[t], preferred_element_type=jnp.float32))
    label_row = jnp.broadcast_to(lab_ref[row:row + 1].astype(jnp.float32), (rows, rows))
    allowed = label_row == label_row.T
    attended = []
    for h in range(width // HEAD_DIM):
        cut = slice(h * HEAD_DIM, (h + 1) * HEAD_DIM)
        query = normalize(projected[0][:, cut], qk_ref[0:1, cut]).astype(jnp.bfloat16)
        key = normalize(projected[1][:, cut], qk_ref[1:2, cut]).astype(jnp.bfloat16)
        value = projected[2][:, cut].astype(jnp.bfloat16)
        score = lax.dot_general(
            query, key, (((1,), (1,)), ((), ())), preferred_element_type=jnp.float32
        ) * HEAD_DIM ** (-0.5)
        exponent = jnp.where(allowed, jnp.exp(score), 0.0)
        weight = exponent * (1.0 / jnp.sum(exponent, axis=1, keepdims=True))
        attended.append(
            jnp.dot(weight.astype(jnp.bfloat16), value, preferred_element_type=jnp.float32)
            .astype(jnp.bfloat16)
        )
    attended = jnp.concatenate(attended, axis=1)
    loads[3].wait()
    for ref, offset in ((o4, 4), (ou3, 3), (od3, -3), (ou2, 2), (od2, -2), (ou1, 1), (od1, -1), (o0, 0)):
        ref[...] = jnp.dot(
            attended, wout[:, columns(offset)], preferred_element_type=jnp.float32
        ).astype(jnp.bfloat16)


def encode(me, labels, row, gain, qk_gain, blocks, slot, w_qkv, w_out):
    n_mp = MESH_MP
    rows, width = blocks[0].shape[0] // 2, blocks[0].shape[1]
    features = n_mp * width
    vmem = pl.BlockSpec(memory_space=pltpu.VMEM)
    hbm = pl.BlockSpec(memory_space=pltpu.HBM)
    return pl.pallas_call(
        functools.partial(encode_kernel, n_mp, slot, row),
        out_shape=[jax.ShapeDtypeStruct((rows, width), jnp.bfloat16)] * 8,
        in_specs=[pl.BlockSpec(memory_space=pltpu.SMEM)] + [vmem] * 3 + [hbm] * 11,
        out_specs=[vmem] * 8,
        scratch_shapes=[
            pltpu.VMEM((n_mp, rows, width), jnp.bfloat16),
            pltpu.VMEM((rows, features), jnp.bfloat16),
            pltpu.VMEM(w_qkv.shape, jnp.bfloat16),
            pltpu.VMEM(w_out.shape, jnp.bfloat16),
            pltpu.SemaphoreType.DMA((12,)),
        ],
        compiler_params=pltpu.CompilerParams(vmem_limit_bytes=VMEM_LIMIT),
        cost_estimate=pl.CostEstimate(
            flops=2 * rows * features * 4 * width,
            bytes_accessed=4 * rows * features,
            transcendentals=0,
        ),
    )(me, labels, gain, qk_gain, *blocks, w_qkv, w_out)


def pack_kernel(kept, labels_smem, labels_ref, patches_hbm, *refs):
    outs, sems = refs[:-1], refs[-1]
    pack_rows = labels_ref.shape[1]
    copies = []
    for k, out in enumerate(outs):
        rows = pl.ds((kept + k) * pack_rows, pack_rows)
        copies.append(
            pltpu.make_async_copy(patches_hbm.at[rows], out.at[pl.ds(0, pack_rows)], sems.at[k])
        )
        copies[-1].start()
    for k, out in enumerate(outs):
        tail = out.shape[0] - pack_rows
        tags = labels_ref[kept + k:kept + k + 1].astype(jnp.float32) + 1.0
        tags = jnp.broadcast_to(tags, (tail, pack_rows)).astype(jnp.bfloat16)
        out[pack_rows:, :pack_rows] = tags
        out[pack_rows:, pack_rows:] = jnp.zeros((tail, out.shape[1] - pack_rows), jnp.bfloat16)
        copies[k].wait()

        @pl.when(labels_smem[kept + k, 0] < 0)
        def _(out=out):
            out[:pack_rows] = jnp.zeros((pack_rows, out.shape[1]), jnp.bfloat16)


def pack_spare(labels, patches, kept, spare):
    pack_rows, width = labels.shape[1], patches.shape[1]
    vmem = pl.BlockSpec(memory_space=pltpu.VMEM)
    return pl.pallas_call(
        functools.partial(pack_kernel, kept),
        out_shape=[jax.ShapeDtypeStruct((pack_rows + 16, width), jnp.bfloat16)] * spare,
        in_specs=[pl.BlockSpec(memory_space=pltpu.SMEM), vmem, pl.BlockSpec(memory_space=pltpu.HBM)],
        out_specs=[vmem] * spare,
        scratch_shapes=[pltpu.SemaphoreType.DMA((spare,))],
        compiler_params=pltpu.CompilerParams(vmem_limit_bytes=SMALL_VMEM),
        cost_estimate=pl.CostEstimate(
            flops=0, bytes_accessed=4 * spare * pack_rows * width, transcendentals=0
        ),
    )(labels, labels, patches)


def merge_kernel(last, labels_smem, labels_ref, patches_hbm, a0, a1, a2, rows_ref, tags_ref, sems):
    pack_rows = labels_ref.shape[1]
    own = labels_smem[last, 0] >= 0
    head = pltpu.make_async_copy(
        patches_hbm.at[pl.ds(0, pack_rows)], rows_ref.at[pl.ds(0, pack_rows)], sems.at[0]
    )
    head.start()

    @pl.when(own)
    def _():
        source = patches_hbm.at[pl.ds(last * pack_rows, pack_rows)]
        copy = pltpu.make_async_copy(source, rows_ref.at[pl.ds(pack_rows, pack_rows)], sems.at[1])
        copy.start()
        copy.wait()
        tags_ref[...] = labels_ref[last:last + 1]

    @pl.when(jnp.logical_not(own))
    def _():
        rows_ref[pack_rows:] = a0[:pack_rows] + a1[:pack_rows] + a2[:pack_rows]
        tags = a0[pack_rows:, :pack_rows] + a1[pack_rows:, :pack_rows] + a2[pack_rows:, :pack_rows]
        tags_ref[...] = tags.astype(jnp.float32)[0:1].astype(jnp.int32) - 1

    head.wait()


def merge_last(labels, patches, arrived, last):
    pack_rows, width = labels.shape[1], patches.shape[1]
    vmem = pl.BlockSpec(memory_space=pltpu.VMEM)
    return pl.pallas_call(
        functools.partial(merge_kernel, last),
        out_shape=[
            jax.ShapeDtypeStruct((2 * pack_rows, width), jnp.bfloat16),
            jax.ShapeDtypeStruct((1, pack_rows), jnp.int32),
        ],
        in_specs=[pl.BlockSpec(memory_space=pltpu.SMEM), vmem, pl.BlockSpec(memory_space=pltpu.HBM)]
        + [vmem] * 3,
        out_specs=[vmem] * 2,
        scratch_shapes=[pltpu.SemaphoreType.DMA((2,))],
        compiler_params=pltpu.CompilerParams(vmem_limit_bytes=SMALL_VMEM),
        cost_estimate=pl.CostEstimate(
            flops=16_000_000_000, bytes_accessed=8 * pack_rows * width, transcendentals=0
        ),
    )(labels, labels, patches, *arrived)


def finish_kernel(labels_smem, x1, x2, xup, xdown, own, up, down, last, r0, r1, r2, out_ref):
    rows = own.shape[0]
    terms = [[own, up, down]]
    for k, ref in enumerate((x1, x2)):
        cut = pl.ds(k * rows, rows)
        terms.append([ref, xup.at[cut], xdown.at[cut]])
    terms += [[last], [r0], [r1], [r2]]
    for pack, parts in enumerate(terms):
        values = sum(part[...].astype(jnp.float32) for part in parts)
        live = labels_smem[pack, 0] >= 0
        out_ref[pack * rows:(pack + 1) * rows] = jnp.where(live, values, 0.0).astype(jnp.bfloat16)


def finish(labels, *parts):
    home_packs, pack_rows = labels.shape
    width = parts[0].shape[1]
    vmem = pl.BlockSpec(memory_space=pltpu.VMEM)
    return pl.pallas_call(
        finish_kernel,
        out_shape=jax.ShapeDtypeStruct((home_packs * pack_rows, width), jnp.bfloat16),
        in_specs=[pl.BlockSpec(memory_space=pltpu.SMEM)] + [vmem] * len(parts),
        out_specs=vmem,
        compiler_params=pltpu.CompilerParams(vmem_limit_bytes=SMALL_VMEM),
        cost_estimate=pl.CostEstimate(
            flops=0, bytes_accessed=4 * home_packs * pack_rows * width, transcendentals=0
        ),
    )(labels, *parts)


class Order:
    def __init__(self, token):
        self.token = token

    def tie(self, *values):
        tied = lax.optimization_barrier(values + (self.token,))[:-1]
        return tied if len(tied) > 1 else tied[0]

    def mark(self, *values):
        self.token = lax.optimization_barrier((self.token,) + values)[0]


class Ring:
    def __init__(self, order):
        size = lax.axis_size("mp")
        self.order = order
        self.up = [(i, (i + 1) % size) for i in range(size)]
        self.down = [(i, (i - 1) % size) for i in range(size)]

    def send(self, rising, falling):
        rising, falling = self.order.tie(rising, falling)
        self.rising = lax.ppermute(rising, "mp", self.up)
        self.falling = lax.ppermute(falling, "mp", self.down)

    def done(self):
        self.order.mark(self.rising, self.falling)


class Gather(Ring):
    def __init__(self, order, block):
        super().__init__(order)
        self.half = block.shape[0] // 2
        self.blocks = [block]
        self.rising = self.falling = block

    def start(self):
        if len(self.blocks) < 7:
            self.send(self.rising, self.falling)
        else:
            self.send(self.rising[:self.half], self.falling[self.half:])

    def done(self):
        super().done()
        self.blocks += [self.rising, self.falling]


def add(first, second):
    return (first.astype(jnp.float32) + second.astype(jnp.float32)).astype(jnp.bfloat16)


def stack(parts):
    return jnp.concatenate(parts, axis=0) if len(parts) > 1 else parts[0]


class Scatter(Ring):
    def __init__(self, order, *packs):
        super().__init__(order)
        self.packs = packs
        self.step = 0

    def begin(self):
        self.send(self.packs[0][7], self.packs[1][7])

    def apart(self):
        chains = [Scatter(self.order, pack) for pack in self.packs]
        chains[0].rising, chains[0].falling = self.rising, None
        chains[1].rising, chains[1].falling = None, self.falling
        return chains

    def start(self):
        up, down = ([pack[5 - 2 * self.step + k] for pack in self.packs] for k in range(2))
        if len(self.packs) == 2 and self.step == 0:
            up[0], down[1] = add(up[0], self.rising), add(down[1], self.falling)
            self.send(stack(up), stack(down))
        else:
            rising, falling = stack(up), stack(down)
            self.send(
                rising if self.rising is None else add(rising, self.rising),
                falling if self.falling is None else add(falling, self.falling),
            )
        self.step += 1

    def terms(self):
        return self.packs[0][0], self.rising, self.falling


def total(ring):
    return sum(term.astype(jnp.float32) for term in ring.terms()).astype(jnp.bfloat16)


def local(patches, labels, ln_gain, w_qkv, qk_gain, w_out):
    groups = lax.axis_size("dp")
    home_packs, pack_rows = labels.shape
    spare = home_packs - WORK_P
    last = WORK_P - 1
    offsets = [1, groups // 2, groups - 1][:spare]
    me = lax.axis_index("mp").astype(jnp.int32).reshape(1)
    gain = ln_gain.reshape(1, -1)
    order = Order(labels[0, :1])

    def over_groups(values, sign):
        return [
            lax.ppermute(value, "dp", [(i, (i + sign * offset) % groups) for i in range(groups)])
            for value, offset in zip(order.tie(*values), offsets)
        ]

    def run(got, tags, row, slot):
        sums = encode(me, tags, row, gain, qk_gain, order.tie(*got.blocks), slot, w_qkv, w_out)
        order.mark(*sums)
        return sums

    def step(ring):
        ring.done()
        ring.start()

    x = Gather(order, patches[pack_rows:last * pack_rows])
    x.start()
    arrived = over_groups(pack_spare(labels, patches, WORK_P, spare), 1)
    step(x)
    order.mark(*arrived)
    rows, last_labels = merge_last(labels, patches, arrived, last)
    y = Gather(order, rows)
    y.start()
    step(x)
    y.done()
    step(x)
    x.done()
    y.start()
    sums1 = run(x, labels, 1, 0)
    step(y)
    sums2 = run(x, labels, 2, 1)
    rx = Scatter(order, sums1, sums2)
    step(y)
    rx.begin()
    y.done()
    step(rx)
    sums3 = run(y, last_labels, 0, 1)
    step(rx)
    sums0 = run(y, labels, 0, 0)
    rx.done()
    ry = Scatter(order, sums0, sums3)
    ry.begin()
    ry.done()
    r0, r3 = ry.apart()
    r3.start()
    r0.start()
    step(r3)
    step(r0)
    step(r3)
    rx.start()
    r3.done()
    sum3 = total(r3)
    returned = over_groups([sum3] * spare, -1)
    step(r0)
    return finish(
        labels, sums1[0], sums2[0], rx.rising, rx.falling, *r0.terms(), sum3, *returned
    )


def solution(mesh):
    placed = (P("dp", "mp"), P("dp", None), P(), P(None, None, "mp"), P(None, "mp"), P("mp", None))
    return jax.shard_map(
        local, mesh=mesh, in_specs=placed, out_specs=P("dp", "mp"), check_vma=False
    )
```

```python
import functools

import jax
import jax.numpy as jnp
from jax import lax
from jax.experimental import pallas as pl
from jax.experimental.pallas import tpu as pltpu
from jax.sharding import PartitionSpec as P

HEAD_DIM = 128
WORK_P = 4
EPSILON = 1e-06
MESH_MP = 8
VMEM_LIMIT = 52 * 1024 * 1024
SMALL_VMEM = 8 * 1024 * 1024


def normalize(values, norm_gain):
    row_mean = jnp.mean(values, axis=-1, keepdims=True)
    centered = values - row_mean
    spread = jnp.mean(centered * centered, axis=-1, keepdims=True)
    return centered * lax.rsqrt(spread + EPSILON) * norm_gain


def encode_kernel(n_mp, slot, row, me_ref, lab_ref, gain_ref, qk_ref, *refs):
    blocks, refs = refs[:9], refs[9:]
    wqkv_hbm, wout_hbm = refs[:2]
    o0, ou1, od1, ou2, od2, ou3, od3 = refs[2:9]
    far, (held, normed, wqkv, wout, sems) = refs[9:-5], refs[-5:]
    rows, width = o0.shape
    features = n_mp * width
    mine = pl.ds(slot * rows, rows)
    sources = [ref.at[mine] for ref in blocks[:7]] + [blocks[7 + slot]]
    fetches = [
        pltpu.make_async_copy(source, held.at[k], sems.at[k]) for k, source in enumerate(sources)
    ]
    loads = [
        pltpu.make_async_copy(wqkv_hbm.at[t], wqkv.at[t], sems.at[8 + t]) for t in range(3)
    ] + [pltpu.make_async_copy(wout_hbm, wout, sems.at[11])]
    for copy in fetches + loads:
        copy.start()
    me = me_ref[0]

    def columns(offset):
        return pl.ds(pl.multiple_of(lax.rem(me + offset + n_mp, n_mp) * width, width), width)

    pieces = [(held.at[k], columns(o)) for k, o in enumerate((0, -1, 1, -2, 2, -3, 3, 4))]

    def folded(part):
        return sum(part[:, c:c + 128] for c in range(0, width, 128))

    sums = jnp.zeros((rows, 128), jnp.float32)
    for (ref, _), copy in zip(pieces, fetches):
        copy.wait()
        sums = sums + folded(ref[...].astype(jnp.float32))
    mean = jnp.sum(sums, axis=1, keepdims=True) * (1.0 / features)
    sums = jnp.zeros((rows, 128), jnp.float32)
    for ref, _ in pieces:
        part = ref[...].astype(jnp.float32) - mean
        sums = sums + folded(part * part)
    spread = jnp.sum(sums, axis=1, keepdims=True) * (1.0 / features)
    scale = lax.rsqrt(spread + EPSILON)
    for ref, cols in pieces:
        part = (ref[...].astype(jnp.float32) - mean) * scale
        normed[:, cols] = (part * gain_ref[0:1, cols]).astype(jnp.bfloat16)

    projected = []
    for t in range(3):
        loads[t].wait()
        projected.append(jnp.dot(normed[...], wqkv[t], preferred_element_type=jnp.float32))
    label_row = jnp.broadcast_to(lab_ref[row:row + 1].astype(jnp.float32), (rows, rows))
    allowed = label_row == label_row.T
    attended = []
    for h in range(width // HEAD_DIM):
        cut = slice(h * HEAD_DIM, (h + 1) * HEAD_DIM)
        query = normalize(projected[0][:, cut], qk_ref[0:1, cut]).astype(jnp.bfloat16)
        key = normalize(projected[1][:, cut], qk_ref[1:2, cut]).astype(jnp.bfloat16)
        value = projected[2][:, cut].astype(jnp.bfloat16)
        score = lax.dot_general(
            query, key, (((1,), (1,)), ((), ())), preferred_element_type=jnp.float32
        ) * HEAD_DIM ** (-0.5)
        exponent = jnp.where(allowed, jnp.exp(score), 0.0)
        weight = exponent * (1.0 / jnp.sum(exponent, axis=1, keepdims=True))
        attended.append(
            jnp.dot(weight.astype(jnp.bfloat16), value, preferred_element_type=jnp.float32)
            .astype(jnp.bfloat16)
        )
    attended = jnp.concatenate(attended, axis=1)
    loads[3].wait()
    out = jnp.dot(attended, wout[:, columns(4)], preferred_element_type=jnp.float32)
    size = rows // len(far)
    for k, ref in enumerate(far):
        ref[...] = out[k * size:(k + 1) * size].astype(jnp.bfloat16)
    for ref, offset in ((ou3, 3), (od3, -3), (ou2, 2), (od2, -2), (ou1, 1), (od1, -1), (o0, 0)):
        ref[...] = jnp.dot(
            attended, wout[:, columns(offset)], preferred_element_type=jnp.float32
        ).astype(jnp.bfloat16)


def encode(me, labels, row, gain, qk_gain, blocks, slot, parts, w_qkv, w_out):
    n_mp = MESH_MP
    rows, width = blocks[0].shape[0] // 2, blocks[0].shape[1]
    features = n_mp * width
    vmem = pl.BlockSpec(memory_space=pltpu.VMEM)
    hbm = pl.BlockSpec(memory_space=pltpu.HBM)
    return pl.pallas_call(
        functools.partial(encode_kernel, n_mp, slot, row),
        out_shape=[jax.ShapeDtypeStruct((rows, width), jnp.bfloat16)] * 7
        + [jax.ShapeDtypeStruct((rows // parts, width), jnp.bfloat16)] * parts,
        in_specs=[pl.BlockSpec(memory_space=pltpu.SMEM)] + [vmem] * 3 + [hbm] * 11,
        out_specs=[vmem] * (7 + parts),
        scratch_shapes=[
            pltpu.VMEM((n_mp, rows, width), jnp.bfloat16),
            pltpu.VMEM((rows, features), jnp.bfloat16),
            pltpu.VMEM(w_qkv.shape, jnp.bfloat16),
            pltpu.VMEM(w_out.shape, jnp.bfloat16),
            pltpu.SemaphoreType.DMA((12,)),
        ],
        compiler_params=pltpu.CompilerParams(vmem_limit_bytes=VMEM_LIMIT),
        cost_estimate=pl.CostEstimate(
            flops=2 * rows * features * 4 * width,
            bytes_accessed=4 * rows * features,
            transcendentals=0,
        ),
    )(me, labels, gain, qk_gain, *blocks, w_qkv, w_out)


def pack_kernel(kept, labels_smem, labels_ref, patches_hbm, *refs):
    outs, sems = refs[:-1], refs[-1]
    pack_rows = labels_ref.shape[1]
    copies = []
    for k, out in enumerate(outs):
        rows = pl.ds((kept + k) * pack_rows, pack_rows)
        copies.append(
            pltpu.make_async_copy(patches_hbm.at[rows], out.at[pl.ds(0, pack_rows)], sems.at[k])
        )
        copies[-1].start()
    for k, out in enumerate(outs):
        tail = out.shape[0] - pack_rows
        tags = labels_ref[kept + k:kept + k + 1].astype(jnp.float32) + 1.0
        tags = jnp.broadcast_to(tags, (tail, pack_rows)).astype(jnp.bfloat16)
        out[pack_rows:, :pack_rows] = tags
        out[pack_rows:, pack_rows:] = jnp.zeros((tail, out.shape[1] - pack_rows), jnp.bfloat16)
        copies[k].wait()

        @pl.when(labels_smem[kept + k, 0] < 0)
        def _(out=out):
            out[:pack_rows] = jnp.zeros((pack_rows, out.shape[1]), jnp.bfloat16)


def pack_spare(labels, patches, kept, spare):
    pack_rows, width = labels.shape[1], patches.shape[1]
    vmem = pl.BlockSpec(memory_space=pltpu.VMEM)
    return pl.pallas_call(
        functools.partial(pack_kernel, kept),
        out_shape=[jax.ShapeDtypeStruct((pack_rows + 16, width), jnp.bfloat16)] * spare,
        in_specs=[pl.BlockSpec(memory_space=pltpu.SMEM), vmem, pl.BlockSpec(memory_space=pltpu.HBM)],
        out_specs=[vmem] * spare,
        scratch_shapes=[pltpu.SemaphoreType.DMA((spare,))],
        compiler_params=pltpu.CompilerParams(vmem_limit_bytes=SMALL_VMEM),
        cost_estimate=pl.CostEstimate(
            flops=0, bytes_accessed=4 * spare * pack_rows * width, transcendentals=0
        ),
    )(labels, labels, patches)


def merge_kernel(last, labels_smem, labels_ref, patches_hbm, a0, a1, a2, rows_ref, tags_ref, sems):
    pack_rows = labels_ref.shape[1]
    own = labels_smem[last, 0] >= 0
    head = pltpu.make_async_copy(
        patches_hbm.at[pl.ds(0, pack_rows)], rows_ref.at[pl.ds(0, pack_rows)], sems.at[0]
    )
    head.start()

    @pl.when(own)
    def _():
        source = patches_hbm.at[pl.ds(last * pack_rows, pack_rows)]
        copy = pltpu.make_async_copy(source, rows_ref.at[pl.ds(pack_rows, pack_rows)], sems.at[1])
        copy.start()
        copy.wait()
        tags_ref[...] = labels_ref[last:last + 1]

    @pl.when(jnp.logical_not(own))
    def _():
        rows_ref[pack_rows:] = a0[:pack_rows] + a1[:pack_rows] + a2[:pack_rows]
        tags = a0[pack_rows:, :pack_rows] + a1[pack_rows:, :pack_rows] + a2[pack_rows:, :pack_rows]
        tags_ref[...] = tags.astype(jnp.float32)[0:1].astype(jnp.int32) - 1

    head.wait()


def merge_last(labels, patches, arrived, last):
    pack_rows, width = labels.shape[1], patches.shape[1]
    vmem = pl.BlockSpec(memory_space=pltpu.VMEM)
    return pl.pallas_call(
        functools.partial(merge_kernel, last),
        out_shape=[
            jax.ShapeDtypeStruct((2 * pack_rows, width), jnp.bfloat16),
            jax.ShapeDtypeStruct((1, pack_rows), jnp.int32),
        ],
        in_specs=[pl.BlockSpec(memory_space=pltpu.SMEM), vmem, pl.BlockSpec(memory_space=pltpu.HBM)]
        + [vmem] * 3,
        out_specs=[vmem] * 2,
        scratch_shapes=[pltpu.SemaphoreType.DMA((2,))],
        compiler_params=pltpu.CompilerParams(vmem_limit_bytes=SMALL_VMEM),
        cost_estimate=pl.CostEstimate(
            flops=16_000_000_000, bytes_accessed=8 * pack_rows * width, transcendentals=0
        ),
    )(labels, labels, patches, *arrived)


def finish_kernel(labels_smem, x1, x2, xup, xdown, own, up, down, last, r0, r1, r2, out_hbm,
                  held, sems):
    rows = own.shape[0]
    terms = [[own, up, down]]
    for k, ref in enumerate((x1, x2)):
        cut = pl.ds(k * rows, rows)
        terms.append([ref, xup.at[cut], xdown.at[cut]])
    terms += [[last], [r0], [r1], [r2]]
    copies = []
    for pack, parts in enumerate(terms):
        values = sum(part[...].astype(jnp.float32) for part in parts)
        live = labels_smem[pack, 0] >= 0
        held[pack] = jnp.where(live, values, 0.0).astype(jnp.bfloat16)
        copies.append(
            pltpu.make_async_copy(
                held.at[pack], out_hbm.at[pl.ds(pack * rows, rows)], sems.at[pack]
            )
        )
        copies[-1].start()
    for copy in copies:
        copy.wait()


def finish(labels, *parts):
    home_packs, pack_rows = labels.shape
    width = parts[0].shape[1]
    vmem = pl.BlockSpec(memory_space=pltpu.VMEM)
    return pl.pallas_call(
        finish_kernel,
        out_shape=jax.ShapeDtypeStruct((home_packs * pack_rows, width), jnp.bfloat16),
        in_specs=[pl.BlockSpec(memory_space=pltpu.SMEM)] + [vmem] * len(parts),
        out_specs=pl.BlockSpec(memory_space=pl.ANY),
        scratch_shapes=[
            pltpu.VMEM((home_packs, pack_rows, width), jnp.bfloat16),
            pltpu.SemaphoreType.DMA((home_packs,)),
        ],
        compiler_params=pltpu.CompilerParams(vmem_limit_bytes=SMALL_VMEM),
        cost_estimate=pl.CostEstimate(
            flops=0, bytes_accessed=4 * home_packs * pack_rows * width, transcendentals=0
        ),
    )(labels, *parts)


class Order:
    def __init__(self, token):
        self.token = token

    def tie(self, *values):
        tied = lax.optimization_barrier(values + (self.token,))[:-1]
        return tied if len(tied) > 1 else tied[0]

    def mark(self, *values):
        self.token = lax.optimization_barrier((self.token,) + values)[0]


class Ring:
    def __init__(self, order):
        size = lax.axis_size("mp")
        self.order = order
        self.up = [(i, (i + 1) % size) for i in range(size)]
        self.down = [(i, (i - 1) % size) for i in range(size)]

    def send(self, rising, falling):
        rising, falling = self.order.tie(rising, falling)
        self.rising = lax.ppermute(rising, "mp", self.up)
        self.falling = lax.ppermute(falling, "mp", self.down)

    def done(self):
        self.order.mark(self.rising, self.falling)


class Gather(Ring):
    def __init__(self, order, block):
        super().__init__(order)
        self.half = block.shape[0] // 2
        self.blocks = [block]
        self.rising = self.falling = block

    def start(self):
        if len(self.blocks) < 7:
            self.send(self.rising, self.falling)
        else:
            self.send(self.rising[:self.half], self.falling[self.half:])

    def done(self):
        super().done()
        self.blocks += [self.rising, self.falling]


def add(first, second):
    return (first.astype(jnp.float32) + second.astype(jnp.float32)).astype(jnp.bfloat16)


def stack(*parts):
    return jnp.concatenate(parts, axis=0) if len(parts) > 1 else parts[0]


class Scatter(Ring):
    def __init__(self, order, *packs):
        super().__init__(order)
        self.packs = packs
        self.rows = packs[0][0].shape[0] * len(packs)
        self.step = 0

    def begin(self):
        self.send(*[part for pack in self.packs for part in pack[7:]])

    def start(self, carried=None):
        up, down = (stack(*[pack[5 - 2 * self.step + k] for pack in self.packs]) for k in range(2))
        rising, falling = self.rising, self.falling
        if self.step == 0:
            rest = self.rows - rising.shape[0]
            rising = jnp.pad(rising, ((0, rest), (0, 0)))
            falling = jnp.pad(falling, ((rest, 0), (0, 0)))
        rising, falling = add(up, rising), add(down, falling)
        if carried is not None:
            half = carried.shape[0] // 2
            rising, falling = stack(rising, carried[:half]), stack(falling, carried[half:])
        self.send(rising, falling)
        self.step += 1

    def part(self, other):
        other.rising, other.falling = self.rising[self.rows:], self.falling[self.rows:]
        self.rising, self.falling = self.rising[:self.rows], self.falling[:self.rows]

    def terms(self):
        return self.packs[0][0], self.rising, self.falling


def total(ring):
    return sum(term.astype(jnp.float32) for term in ring.terms()).astype(jnp.bfloat16)


def local(patches, labels, ln_gain, w_qkv, qk_gain, w_out):
    groups = lax.axis_size("dp")
    home_packs, pack_rows = labels.shape
    spare = home_packs - WORK_P
    last = WORK_P - 1
    offsets = [1, groups // 2, groups - 1][:spare]
    me = lax.axis_index("mp").astype(jnp.int32).reshape(1)
    gain = ln_gain.reshape(1, -1)
    order = Order(labels[0, :1])

    def over_groups(values, sign):
        return [
            lax.ppermute(value, "dp", [(i, (i + sign * offset) % groups) for i in range(groups)])
            for value, offset in zip(order.tie(*values), offsets)
        ]

    def run(got, tags, row, slot, parts=1):
        blocks = order.tie(*got.blocks)
        sums = encode(me, tags, row, gain, qk_gain, blocks, slot, parts, w_qkv, w_out)
        order.mark(*sums)
        return sums

    def step(ring):
        ring.done()
        ring.start()

    x = Gather(order, patches[pack_rows:last * pack_rows])
    x.start()
    arrived = over_groups(pack_spare(labels, patches, WORK_P, spare), 1)
    step(x)
    order.mark(*arrived)
    rows, last_labels = merge_last(labels, patches, arrived, last)
    y = Gather(order, rows)
    y.start()
    step(x)
    y.done()
    step(x)
    x.done()
    y.start()
    sums1 = run(x, labels, 1, 0)
    step(y)
    sums2 = run(x, labels, 2, 1)
    rx = Scatter(order, sums1, sums2)
    step(y)
    rx.begin()
    y.done()
    step(rx)
    sums3 = run(y, last_labels, 0, 1)
    r3 = Scatter(order, sums3)
    rx.done()
    rx.start(sums3[7])
    r0 = Scatter(order, run(y, labels, 0, 0, 2))
    rx.done()
    rx.part(r3)
    r3.start()
    r0.begin()
    step(r3)
    step(r0)
    rx.start()
    step(r3)
    step(r0)
    r3.done()
    sum3 = total(r3)
    returned = over_groups([sum3] * spare, -1)
    step(r0)
    return finish(
        labels, sums1[0], sums2[0], rx.rising, rx.falling, *r0.terms(), sum3, *returned
    )


def solution(mesh):
    placed = (P("dp", "mp"), P("dp", None), P(), P(None, None, "mp"), P(None, "mp"), P("mp", None))
    return jax.shard_map(
        local, mesh=mesh, in_specs=placed, out_specs=P("dp", "mp"), check_vma=False
    )
```

```python
import functools

import jax
import jax.numpy as jnp
from jax import lax
from jax.experimental import pallas as pl
from jax.experimental.pallas import tpu as pltpu
from jax.sharding import PartitionSpec as P

HEAD_DIM = 128
WORK_P = 4
EPSILON = 1e-06
MESH_MP = 8
VMEM_LIMIT = 52 * 1024 * 1024
SMALL_VMEM = 8 * 1024 * 1024


def normalize(values, norm_gain):
    row_mean = jnp.mean(values, axis=-1, keepdims=True)
    centered = values - row_mean
    spread = jnp.mean(centered * centered, axis=-1, keepdims=True)
    return centered * lax.rsqrt(spread + EPSILON) * norm_gain


def encode_kernel(n_mp, slots, slot, row, me_ref, lab_ref, gain_ref, qk_ref, *refs):
    blocks, refs = refs[:9], refs[9:]
    wqkv_hbm, wout_hbm = refs[:2]
    o0, ou1, od1, ou2, od2, ou3, od3 = refs[2:9]
    far, (held, normed, wqkv, wout, sems) = refs[9:-5], refs[-5:]
    rows, width = o0.shape
    features = n_mp * width
    mine = pl.ds(slot * rows, rows)
    half = rows // 2
    moves = [(ref.at[mine], held.at[k]) for k, ref in enumerate(blocks[:7])]
    if slots == 1:
        moves += [(blocks[7 + k], held.at[7, pl.ds(k * half, half)]) for k in range(2)]
    else:
        moves.append((blocks[7 + slot], held.at[7]))
    fetches = [
        pltpu.make_async_copy(source, target, sems.at[k])
        for k, (source, target) in enumerate(moves)
    ]
    loads = [
        pltpu.make_async_copy(wqkv_hbm.at[t], wqkv.at[t], sems.at[9 + t]) for t in range(3)
    ] + [pltpu.make_async_copy(wout_hbm, wout, sems.at[12])]
    for copy in fetches + loads:
        copy.start()
    me = me_ref[0]

    def columns(offset):
        return pl.ds(pl.multiple_of(lax.rem(me + offset + n_mp, n_mp) * width, width), width)

    pieces = [(held.at[k], columns(o)) for k, o in enumerate((0, -1, 1, -2, 2, -3, 3, 4))]

    def folded(part):
        return sum(part[:, c:c + 128] for c in range(0, width, 128))

    sums = jnp.zeros((rows, 128), jnp.float32)
    for copy in fetches:
        copy.wait()
    for ref, _ in pieces:
        sums = sums + folded(ref[...].astype(jnp.float32))
    mean = jnp.sum(sums, axis=1, keepdims=True) * (1.0 / features)
    sums = jnp.zeros((rows, 128), jnp.float32)
    for ref, _ in pieces:
        part = ref[...].astype(jnp.float32) - mean
        sums = sums + folded(part * part)
    spread = jnp.sum(sums, axis=1, keepdims=True) * (1.0 / features)
    scale = lax.rsqrt(spread + EPSILON)
    for ref, cols in pieces:
        part = (ref[...].astype(jnp.float32) - mean) * scale
        normed[:, cols] = (part * gain_ref[0:1, cols]).astype(jnp.bfloat16)

    projected = []
    for t in range(3):
        loads[t].wait()
        projected.append(jnp.dot(normed[...], wqkv[t], preferred_element_type=jnp.float32))
    label_row = jnp.broadcast_to(lab_ref[row:row + 1].astype(jnp.float32), (rows, rows))
    allowed = label_row == label_row.T
    attended = []
    for h in range(width // HEAD_DIM):
        cut = slice(h * HEAD_DIM, (h + 1) * HEAD_DIM)
        query = normalize(projected[0][:, cut], qk_ref[0:1, cut]).astype(jnp.bfloat16)
        key = normalize(projected[1][:, cut], qk_ref[1:2, cut]).astype(jnp.bfloat16)
        value = projected[2][:, cut].astype(jnp.bfloat16)
        score = lax.dot_general(
            query, key, (((1,), (1,)), ((), ())), preferred_element_type=jnp.float32
        ) * HEAD_DIM ** (-0.5)
        exponent = jnp.where(allowed, jnp.exp(score), 0.0)
        weight = exponent * (1.0 / jnp.sum(exponent, axis=1, keepdims=True))
        attended.append(
            jnp.dot(weight.astype(jnp.bfloat16), value, preferred_element_type=jnp.float32)
            .astype(jnp.bfloat16)
        )
    attended = jnp.concatenate(attended, axis=1)
    loads[3].wait()
    out = jnp.dot(attended, wout[:, columns(4)], preferred_element_type=jnp.float32)
    size = rows // len(far)
    for k, ref in enumerate(far):
        ref[...] = out[k * size:(k + 1) * size].astype(jnp.bfloat16)
    for ref, offset in ((ou3, 3), (od3, -3), (ou2, 2), (od2, -2), (ou1, 1), (od1, -1), (o0, 0)):
        ref[...] = jnp.dot(
            attended, wout[:, columns(offset)], preferred_element_type=jnp.float32
        ).astype(jnp.bfloat16)


def encode(me, labels, row, gain, qk_gain, blocks, slot, slots, parts, w_qkv, w_out):
    n_mp = MESH_MP
    rows, width = blocks[0].shape[0] // slots, blocks[0].shape[1]
    features = n_mp * width
    vmem = pl.BlockSpec(memory_space=pltpu.VMEM)
    hbm = pl.BlockSpec(memory_space=pltpu.HBM)
    return pl.pallas_call(
        functools.partial(encode_kernel, n_mp, slots, slot, row),
        out_shape=[jax.ShapeDtypeStruct((rows, width), jnp.bfloat16)] * 7
        + [jax.ShapeDtypeStruct((rows // parts, width), jnp.bfloat16)] * parts,
        in_specs=[pl.BlockSpec(memory_space=pltpu.SMEM)] + [vmem] * 3 + [hbm] * 11,
        out_specs=[vmem] * (7 + parts),
        scratch_shapes=[
            pltpu.VMEM((n_mp, rows, width), jnp.bfloat16),
            pltpu.VMEM((rows, features), jnp.bfloat16),
            pltpu.VMEM(w_qkv.shape, jnp.bfloat16),
            pltpu.VMEM(w_out.shape, jnp.bfloat16),
            pltpu.SemaphoreType.DMA((13,)),
        ],
        compiler_params=pltpu.CompilerParams(vmem_limit_bytes=VMEM_LIMIT),
        cost_estimate=pl.CostEstimate(
            flops=2 * rows * features * 4 * width,
            bytes_accessed=4 * rows * features,
            transcendentals=0,
        ),
    )(me, labels, gain, qk_gain, *blocks, w_qkv, w_out)


def pack_kernel(kept, labels_smem, labels_ref, patches_hbm, *refs):
    outs, sems = refs[:-1], refs[-1]
    pack_rows = labels_ref.shape[1]
    copies = []
    for k, out in enumerate(outs):
        rows = pl.ds((kept + k) * pack_rows, pack_rows)
        copies.append(
            pltpu.make_async_copy(patches_hbm.at[rows], out.at[pl.ds(0, pack_rows)], sems.at[k])
        )
        copies[-1].start()
    for k, out in enumerate(outs):
        tail = out.shape[0] - pack_rows
        tags = labels_ref[kept + k:kept + k + 1].astype(jnp.float32) + 1.0
        tags = jnp.broadcast_to(tags, (tail, pack_rows)).astype(jnp.bfloat16)
        out[pack_rows:, :pack_rows] = tags
        out[pack_rows:, pack_rows:] = jnp.zeros((tail, out.shape[1] - pack_rows), jnp.bfloat16)
        copies[k].wait()

        @pl.when(labels_smem[kept + k, 0] < 0)
        def _(out=out):
            out[:pack_rows] = jnp.zeros((pack_rows, out.shape[1]), jnp.bfloat16)


def pack_spare(labels, patches, kept, spare):
    pack_rows, width = labels.shape[1], patches.shape[1]
    vmem = pl.BlockSpec(memory_space=pltpu.VMEM)
    return pl.pallas_call(
        functools.partial(pack_kernel, kept),
        out_shape=[jax.ShapeDtypeStruct((pack_rows + 16, width), jnp.bfloat16)] * spare,
        in_specs=[pl.BlockSpec(memory_space=pltpu.SMEM), vmem, pl.BlockSpec(memory_space=pltpu.HBM)],
        out_specs=[vmem] * spare,
        scratch_shapes=[pltpu.SemaphoreType.DMA((spare,))],
        compiler_params=pltpu.CompilerParams(vmem_limit_bytes=SMALL_VMEM),
        cost_estimate=pl.CostEstimate(
            flops=0, bytes_accessed=4 * spare * pack_rows * width, transcendentals=0
        ),
    )(labels, labels, patches)


def merge_kernel(last, labels_smem, labels_ref, patches_hbm, a0, a1, a2, rows_ref, tags_ref, sem):
    pack_rows = labels_ref.shape[1]
    own = labels_smem[last, 0] >= 0

    @pl.when(own)
    def _():
        source = patches_hbm.at[pl.ds(last * pack_rows, pack_rows)]
        copy = pltpu.make_async_copy(source, rows_ref, sem)
        copy.start()
        copy.wait()
        tags_ref[...] = labels_ref[last:last + 1]

    @pl.when(jnp.logical_not(own))
    def _():
        rows_ref[...] = a0[:pack_rows] + a1[:pack_rows] + a2[:pack_rows]
        tags = a0[pack_rows:, :pack_rows] + a1[pack_rows:, :pack_rows] + a2[pack_rows:, :pack_rows]
        tags_ref[...] = tags.astype(jnp.float32)[0:1].astype(jnp.int32) - 1


def merge_last(labels, patches, arrived, last):
    pack_rows, width = labels.shape[1], patches.shape[1]
    vmem = pl.BlockSpec(memory_space=pltpu.VMEM)
    return pl.pallas_call(
        functools.partial(merge_kernel, last),
        out_shape=[
            jax.ShapeDtypeStruct((pack_rows, width), jnp.bfloat16),
            jax.ShapeDtypeStruct((1, pack_rows), jnp.int32),
        ],
        in_specs=[pl.BlockSpec(memory_space=pltpu.SMEM), vmem, pl.BlockSpec(memory_space=pl.ANY)]
        + [vmem] * 3,
        out_specs=[vmem] * 2,
        scratch_shapes=[pltpu.SemaphoreType.DMA(())],
        compiler_params=pltpu.CompilerParams(vmem_limit_bytes=SMALL_VMEM),
        cost_estimate=pl.CostEstimate(
            flops=16_000_000_000, bytes_accessed=8 * pack_rows * width, transcendentals=0
        ),
    )(labels, labels, patches, *arrived)


def finish_kernel(labels_smem, x1, x2, xup, xdown, own, up, down, last, r0, r1, r2, out_hbm,
                  held, sems):
    rows = own.shape[0]
    terms = [[own, up, down]]
    for k, ref in enumerate((x1, x2)):
        cut = pl.ds(k * rows, rows)
        terms.append([ref, xup.at[cut], xdown.at[cut]])
    terms += [[last], [r0], [r1], [r2]]
    copies = []
    for pack, parts in enumerate(terms):
        values = sum(part[...].astype(jnp.float32) for part in parts)
        live = labels_smem[pack, 0] >= 0
        held[pack] = jnp.where(live, values, 0.0).astype(jnp.bfloat16)
        copies.append(
            pltpu.make_async_copy(
                held.at[pack], out_hbm.at[pl.ds(pack * rows, rows)], sems.at[pack]
            )
        )
        copies[-1].start()
    for copy in copies:
        copy.wait()


def finish(labels, *parts):
    home_packs, pack_rows = labels.shape
    width = parts[0].shape[1]
    vmem = pl.BlockSpec(memory_space=pltpu.VMEM)
    return pl.pallas_call(
        finish_kernel,
        out_shape=jax.ShapeDtypeStruct((home_packs * pack_rows, width), jnp.bfloat16),
        in_specs=[pl.BlockSpec(memory_space=pltpu.SMEM)] + [vmem] * len(parts),
        out_specs=pl.BlockSpec(memory_space=pl.ANY),
        scratch_shapes=[
            pltpu.VMEM((home_packs, pack_rows, width), jnp.bfloat16),
            pltpu.SemaphoreType.DMA((home_packs,)),
        ],
        compiler_params=pltpu.CompilerParams(vmem_limit_bytes=SMALL_VMEM),
        cost_estimate=pl.CostEstimate(
            flops=0, bytes_accessed=4 * home_packs * pack_rows * width, transcendentals=0
        ),
    )(labels, *parts)


class Order:
    def __init__(self, token):
        self.token = token

    def tie(self, *values):
        tied = lax.optimization_barrier(values + (self.token,))[:-1]
        return tied if len(tied) > 1 else tied[0]

    def mark(self, *values):
        self.token = lax.optimization_barrier((self.token,) + values)[0]


class Ring:
    def __init__(self, order):
        size = lax.axis_size("mp")
        self.order = order
        self.up = [(i, (i + 1) % size) for i in range(size)]
        self.down = [(i, (i - 1) % size) for i in range(size)]

    def send(self, rising, falling):
        rising, falling = self.order.tie(rising, falling)
        self.rising = lax.ppermute(rising, "mp", self.up)
        self.falling = lax.ppermute(falling, "mp", self.down)

    def done(self):
        self.order.mark(self.rising, self.falling)


class Gather(Ring):
    def __init__(self, order, block):
        super().__init__(order)
        self.half = block.shape[0] // 2
        self.blocks = [block]
        self.rising = self.falling = block

    def start(self):
        if len(self.blocks) < 7:
            self.send(self.rising, self.falling)
        else:
            self.send(self.rising[:self.half], self.falling[self.half:])

    def done(self):
        super().done()
        self.blocks += [self.rising, self.falling]


def add(first, second):
    return (first.astype(jnp.float32) + second.astype(jnp.float32)).astype(jnp.bfloat16)


def stack(*parts):
    return jnp.concatenate(parts, axis=0) if len(parts) > 1 else parts[0]


class Scatter(Ring):
    def __init__(self, order, *packs):
        super().__init__(order)
        self.packs = packs
        self.rows = packs[0][0].shape[0] * len(packs)
        self.step = 0

    def begin(self):
        self.send(*[part for pack in self.packs for part in pack[7:]])

    def start(self, carried=None):
        up, down = (stack(*[pack[5 - 2 * self.step + k] for pack in self.packs]) for k in range(2))
        rising, falling = self.rising, self.falling
        if self.step == 0:
            rest = self.rows - rising.shape[0]
            rising = jnp.pad(rising, ((0, rest), (0, 0)))
            falling = jnp.pad(falling, ((rest, 0), (0, 0)))
        rising, falling = add(up, rising), add(down, falling)
        if carried is not None:
            half = carried.shape[0] // 2
            rising, falling = stack(rising, carried[:half]), stack(falling, carried[half:])
        self.send(rising, falling)
        self.step += 1

    def part(self, other):
        other.rising, other.falling = self.rising[self.rows:], self.falling[self.rows:]
        self.rising, self.falling = self.rising[:self.rows], self.falling[:self.rows]

    def terms(self):
        return self.packs[0][0], self.rising, self.falling


def total(ring):
    return sum(term.astype(jnp.float32) for term in ring.terms()).astype(jnp.bfloat16)


def local(patches, labels, ln_gain, w_qkv, qk_gain, w_out):
    groups = lax.axis_size("dp")
    home_packs, pack_rows = labels.shape
    spare = home_packs - WORK_P
    last = WORK_P - 1
    offsets = [1, groups // 2, groups - 1][:spare]
    me = lax.axis_index("mp").astype(jnp.int32).reshape(1)
    gain = ln_gain.reshape(1, -1)
    order = Order(labels[0, :1])

    def over_groups(values, sign):
        return [
            lax.ppermute(value, "dp", [(i, (i + sign * offset) % groups) for i in range(groups)])
            for value, offset in zip(order.tie(*values), offsets)
        ]

    def run(got, tags, row, slot=0, slots=1, parts=1):
        blocks = order.tie(*got.blocks)
        sums = encode(me, tags, row, gain, qk_gain, blocks, slot, slots, parts, w_qkv, w_out)
        order.mark(*sums)
        return sums

    def step(ring):
        ring.done()
        ring.start()

    x = Gather(order, patches[pack_rows:last * pack_rows])
    a = Gather(order, patches[:pack_rows])
    x.start()
    a.start()
    arrived = over_groups(pack_spare(labels, patches, WORK_P, spare), 1)
    step(x)
    step(a)
    order.mark(*arrived)
    rows, last_labels = merge_last(labels, patches, arrived, last)
    order.mark(rows)
    c = Gather(order, rows)
    c.start()
    step(x)
    step(a)
    c.done()
    step(x)
    a.done()
    x.done()
    c.start()
    a.start()
    sums1 = run(x, labels, 1, 0, 2)
    a.done()
    step(c)
    sums2 = run(x, labels, 2, 1, 2)
    rx = Scatter(order, sums1, sums2)
    step(c)
    rx.begin()
    sums0 = run(a, labels, 0)
    c.done()
    rx.done()
    rx.start(sums0[7])
    r0 = Scatter(order, sums0)
    r3 = Scatter(order, run(c, last_labels, 0, parts=2))
    rx.done()
    rx.part(r0)
    r3.begin()
    r0.start()
    rx.start()
    step(r3)
    step(r0)
    step(r3)
    rx.done()
    rx.start()
    step(r0)
    step(r3)
    r3.done()
    sum3 = total(r3)
    returned = over_groups([sum3] * spare, -1)
    return finish(
        labels, sums1[0], sums2[0], rx.rising, rx.falling, *r0.terms(), sum3, *returned
    )


def solution(mesh):
    placed = (P("dp", "mp"), P("dp", None), P(), P(None, None, "mp"), P(None, "mp"), P("mp", None))
    return jax.shard_map(
        local, mesh=mesh, in_specs=placed, out_specs=P("dp", "mp"), check_vma=False
    )
```

```python
import functools

import jax
import jax.numpy as jnp
from jax import lax
from jax.experimental import pallas as pl
from jax.experimental.pallas import tpu as pltpu
from jax.sharding import PartitionSpec as P

HEAD_DIM = 128
WORK_P = 4
EPSILON = 1e-06
MESH_MP = 8
VMEM_LIMIT = 52 * 1024 * 1024
SMALL_VMEM = 8 * 1024 * 1024


def normalize(values, norm_gain):
    row_mean = jnp.mean(values, axis=-1, keepdims=True)
    centered = values - row_mean
    spread = jnp.mean(centered * centered, axis=-1, keepdims=True)
    return centered * lax.rsqrt(spread + EPSILON) * norm_gain


def encode_kernel(n_mp, slot, row, me_ref, lab_ref, gain_ref, qk_ref, *refs):
    blocks, refs = refs[:9], refs[9:]
    wqkv_hbm, wout_hbm = refs[:2]
    o0, ou1, od1, ou2, od2, ou3, od3 = refs[2:9]
    far, (held, normed, wqkv, wout, sems) = refs[9:-5], refs[-5:]
    rows, width = o0.shape
    features = n_mp * width
    mine = pl.ds(slot * rows, rows)
    sources = [ref.at[mine] for ref in blocks[:7]] + [blocks[7 + slot]]
    fetches = [
        pltpu.make_async_copy(source, held.at[k], sems.at[k]) for k, source in enumerate(sources)
    ]
    loads = [
        pltpu.make_async_copy(wqkv_hbm.at[t], wqkv.at[t], sems.at[8 + t]) for t in range(3)
    ] + [pltpu.make_async_copy(wout_hbm, wout, sems.at[11])]
    for copy in fetches + loads:
        copy.start()
    me = me_ref[0]

    def columns(offset):
        return pl.ds(pl.multiple_of(lax.rem(me + offset + n_mp, n_mp) * width, width), width)

    pieces = [(held.at[k], columns(o)) for k, o in enumerate((0, -1, 1, -2, 2, -3, 3, 4))]

    def folded(part):
        return sum(part[:, c:c + 128] for c in range(0, width, 128))

    sums = jnp.zeros((rows, 128), jnp.float32)
    for (ref, _), copy in zip(pieces, fetches):
        copy.wait()
        sums = sums + folded(ref[...].astype(jnp.float32))
    mean = jnp.sum(sums, axis=1, keepdims=True) * (1.0 / features)
    sums = jnp.zeros((rows, 128), jnp.float32)
    for ref, _ in pieces:
        part = ref[...].astype(jnp.float32) - mean
        sums = sums + folded(part * part)
    spread = jnp.sum(sums, axis=1, keepdims=True) * (1.0 / features)
    scale = lax.rsqrt(spread + EPSILON)
    for ref, cols in pieces:
        part = (ref[...].astype(jnp.float32) - mean) * scale
        normed[:, cols] = (part * gain_ref[0:1, cols]).astype(jnp.bfloat16)

    projected = []
    for t in range(3):
        loads[t].wait()
        projected.append(jnp.dot(normed[...], wqkv[t], preferred_element_type=jnp.float32))
    label_row = jnp.broadcast_to(lab_ref[row:row + 1].astype(jnp.float32), (rows, rows))
    allowed = label_row == label_row.T
    attended = []
    for h in range(width // HEAD_DIM):
        cut = slice(h * HEAD_DIM, (h + 1) * HEAD_DIM)
        query = normalize(projected[0][:, cut], qk_ref[0:1, cut]).astype(jnp.bfloat16)
        key = normalize(projected[1][:, cut], qk_ref[1:2, cut]).astype(jnp.bfloat16)
        value = projected[2][:, cut].astype(jnp.bfloat16)
        score = lax.dot_general(
            query, key, (((1,), (1,)), ((), ())), preferred_element_type=jnp.float32
        ) * HEAD_DIM ** (-0.5)
        exponent = jnp.where(allowed, jnp.exp(score), 0.0)
        weight = exponent * (1.0 / jnp.sum(exponent, axis=1, keepdims=True))
        attended.append(
            jnp.dot(weight.astype(jnp.bfloat16), value, preferred_element_type=jnp.float32)
            .astype(jnp.bfloat16)
        )
    attended = jnp.concatenate(attended, axis=1)
    loads[3].wait()
    out = jnp.dot(attended, wout[:, columns(4)], preferred_element_type=jnp.float32)
    size = rows // len(far)
    for k, ref in enumerate(far):
        ref[...] = out[k * size:(k + 1) * size].astype(jnp.bfloat16)
    for ref, offset in ((ou3, 3), (od3, -3), (ou2, 2), (od2, -2), (ou1, 1), (od1, -1), (o0, 0)):
        ref[...] = jnp.dot(
            attended, wout[:, columns(offset)], preferred_element_type=jnp.float32
        ).astype(jnp.bfloat16)


def encode(me, labels, row, gain, qk_gain, blocks, slot, parts, w_qkv, w_out):
    n_mp = MESH_MP
    rows, width = blocks[0].shape[0] // 2, blocks[0].shape[1]
    features = n_mp * width
    vmem = pl.BlockSpec(memory_space=pltpu.VMEM)
    hbm = pl.BlockSpec(memory_space=pltpu.HBM)
    return pl.pallas_call(
        functools.partial(encode_kernel, n_mp, slot, row),
        out_shape=[jax.ShapeDtypeStruct((rows, width), jnp.bfloat16)] * 7
        + [jax.ShapeDtypeStruct((rows // parts, width), jnp.bfloat16)] * parts,
        in_specs=[pl.BlockSpec(memory_space=pltpu.SMEM)] + [vmem] * 3 + [hbm] * 11,
        out_specs=[vmem] * (7 + parts),
        scratch_shapes=[
            pltpu.VMEM((n_mp, rows, width), jnp.bfloat16),
            pltpu.VMEM((rows, features), jnp.bfloat16),
            pltpu.VMEM(w_qkv.shape, jnp.bfloat16),
            pltpu.VMEM(w_out.shape, jnp.bfloat16),
            pltpu.SemaphoreType.DMA((12,)),
        ],
        compiler_params=pltpu.CompilerParams(vmem_limit_bytes=VMEM_LIMIT),
        cost_estimate=pl.CostEstimate(
            flops=2 * rows * features * 4 * width,
            bytes_accessed=4 * rows * features,
            transcendentals=0,
        ),
    )(me, labels, gain, qk_gain, *blocks, w_qkv, w_out)


def pack_kernel(kept, labels_smem, labels_ref, patches_hbm, *refs):
    outs, sems = refs[:-1], refs[-1]
    pack_rows = labels_ref.shape[1]
    copies = []
    for k, out in enumerate(outs):
        rows = pl.ds((kept + k) * pack_rows, pack_rows)
        copies.append(
            pltpu.make_async_copy(patches_hbm.at[rows], out.at[pl.ds(0, pack_rows)], sems.at[k])
        )
        copies[-1].start()
    for k, out in enumerate(outs):
        tail = out.shape[0] - pack_rows
        tags = labels_ref[kept + k:kept + k + 1].astype(jnp.float32) + 1.0
        tags = jnp.broadcast_to(tags, (tail, pack_rows)).astype(jnp.bfloat16)
        out[pack_rows:, :pack_rows] = tags
        out[pack_rows:, pack_rows:] = jnp.zeros((tail, out.shape[1] - pack_rows), jnp.bfloat16)
        copies[k].wait()

        @pl.when(labels_smem[kept + k, 0] < 0)
        def _(out=out):
            out[:pack_rows] = jnp.zeros((pack_rows, out.shape[1]), jnp.bfloat16)


def pack_spare(labels, patches, kept, spare):
    pack_rows, width = labels.shape[1], patches.shape[1]
    vmem = pl.BlockSpec(memory_space=pltpu.VMEM)
    return pl.pallas_call(
        functools.partial(pack_kernel, kept),
        out_shape=[jax.ShapeDtypeStruct((pack_rows + 16, width), jnp.bfloat16)] * spare,
        in_specs=[pl.BlockSpec(memory_space=pltpu.SMEM), vmem, pl.BlockSpec(memory_space=pltpu.HBM)],
        out_specs=[vmem] * spare,
        scratch_shapes=[pltpu.SemaphoreType.DMA((spare,))],
        compiler_params=pltpu.CompilerParams(vmem_limit_bytes=SMALL_VMEM),
        cost_estimate=pl.CostEstimate(
            flops=0, bytes_accessed=4 * spare * pack_rows * width, transcendentals=0
        ),
    )(labels, labels, patches)


def merge_kernel(last, labels_smem, labels_ref, patches_hbm, a0, a1, a2, rows_ref, tags_ref, sems):
    pack_rows = labels_ref.shape[1]
    own = labels_smem[last, 0] >= 0
    head = pltpu.make_async_copy(
        patches_hbm.at[pl.ds(0, pack_rows)], rows_ref.at[pl.ds(0, pack_rows)], sems.at[0]
    )
    head.start()

    @pl.when(own)
    def _():
        source = patches_hbm.at[pl.ds(last * pack_rows, pack_rows)]
        copy = pltpu.make_async_copy(source, rows_ref.at[pl.ds(pack_rows, pack_rows)], sems.at[1])
        copy.start()
        copy.wait()
        tags_ref[...] = labels_ref[last:last + 1]

    @pl.when(jnp.logical_not(own))
    def _():
        rows_ref[pack_rows:] = a0[:pack_rows] + a1[:pack_rows] + a2[:pack_rows]
        tags = a0[pack_rows:, :pack_rows] + a1[pack_rows:, :pack_rows] + a2[pack_rows:, :pack_rows]
        tags_ref[...] = tags.astype(jnp.float32)[0:1].astype(jnp.int32) - 1

    head.wait()


def merge_last(labels, patches, arrived, last):
    pack_rows, width = labels.shape[1], patches.shape[1]
    vmem = pl.BlockSpec(memory_space=pltpu.VMEM)
    return pl.pallas_call(
        functools.partial(merge_kernel, last),
        out_shape=[
            jax.ShapeDtypeStruct((2 * pack_rows, width), jnp.bfloat16),
            jax.ShapeDtypeStruct((1, pack_rows), jnp.int32),
        ],
        in_specs=[pl.BlockSpec(memory_space=pltpu.SMEM), vmem, pl.BlockSpec(memory_space=pltpu.HBM)]
        + [vmem] * 3,
        out_specs=[vmem] * 2,
        scratch_shapes=[pltpu.SemaphoreType.DMA((2,))],
        compiler_params=pltpu.CompilerParams(vmem_limit_bytes=SMALL_VMEM),
        cost_estimate=pl.CostEstimate(
            flops=16_000_000_000, bytes_accessed=8 * pack_rows * width, transcendentals=0
        ),
    )(labels, labels, patches, *arrived)


def finish_kernel(labels_smem, x1, x2, xup, xdown, own, up, down, last, r1, r0, r2, out_hbm,
                  held, sems):
    rows = own.shape[0]
    terms = [[own, up, down]]
    for k, ref in enumerate((x1, x2)):
        cut = pl.ds(k * rows, rows)
        terms.append([ref, xup.at[cut], xdown.at[cut]])
    terms += [[last], [r0], [r1], [r2]]
    copies = []
    for pack, parts in enumerate(terms):
        values = sum(part[...].astype(jnp.float32) for part in parts)
        live = labels_smem[pack, 0] >= 0
        held[pack] = jnp.where(live, values, 0.0).astype(jnp.bfloat16)
        copies.append(
            pltpu.make_async_copy(
                held.at[pack], out_hbm.at[pl.ds(pack * rows, rows)], sems.at[pack]
            )
        )
        copies[-1].start()
    for copy in copies:
        copy.wait()


def finish(labels, *parts):
    home_packs, pack_rows = labels.shape
    width = parts[0].shape[1]
    vmem = pl.BlockSpec(memory_space=pltpu.VMEM)
    return pl.pallas_call(
        finish_kernel,
        out_shape=jax.ShapeDtypeStruct((home_packs * pack_rows, width), jnp.bfloat16),
        in_specs=[pl.BlockSpec(memory_space=pltpu.SMEM)] + [vmem] * len(parts),
        out_specs=pl.BlockSpec(memory_space=pl.ANY),
        scratch_shapes=[
            pltpu.VMEM((home_packs, pack_rows, width), jnp.bfloat16),
            pltpu.SemaphoreType.DMA((home_packs,)),
        ],
        compiler_params=pltpu.CompilerParams(vmem_limit_bytes=SMALL_VMEM),
        cost_estimate=pl.CostEstimate(
            flops=0, bytes_accessed=4 * home_packs * pack_rows * width, transcendentals=0
        ),
    )(labels, *parts)


class Order:
    def __init__(self, token):
        self.token = token

    def tie(self, *values):
        tied = lax.optimization_barrier(values + (self.token,))[:-1]
        return tied if len(tied) > 1 else tied[0]

    def mark(self, *values):
        self.token = lax.optimization_barrier((self.token,) + values)[0]


class Ring:
    def __init__(self, order):
        size = lax.axis_size("mp")
        self.order = order
        self.up = [(i, (i + 1) % size) for i in range(size)]
        self.down = [(i, (i - 1) % size) for i in range(size)]

    def send(self, rising, falling):
        rising, falling = self.order.tie(rising, falling)
        self.rising = lax.ppermute(rising, "mp", self.up)
        self.falling = lax.ppermute(falling, "mp", self.down)

    def done(self):
        self.order.mark(self.rising, self.falling)


class Gather(Ring):
    def __init__(self, order, block):
        super().__init__(order)
        self.half = block.shape[0] // 2
        self.blocks = [block]
        self.rising = self.falling = block

    def start(self):
        if len(self.blocks) < 7:
            self.send(self.rising, self.falling)
        else:
            self.send(self.rising[:self.half], self.falling[self.half:])

    def done(self):
        super().done()
        self.blocks += [self.rising, self.falling]


def add(first, second):
    return (first.astype(jnp.float32) + second.astype(jnp.float32)).astype(jnp.bfloat16)


def stack(*parts):
    return jnp.concatenate(parts, axis=0) if len(parts) > 1 else parts[0]


class Scatter(Ring):
    def __init__(self, order, *packs):
        super().__init__(order)
        self.packs = packs
        self.rows = packs[0][0].shape[0] * len(packs)
        self.step = 0

    def begin(self):
        self.send(*[part for pack in self.packs for part in pack[7:]])

    def start(self, carried=None):
        up, down = (stack(*[pack[5 - 2 * self.step + k] for pack in self.packs]) for k in range(2))
        rising, falling = self.rising, self.falling
        if self.step == 0:
            rest = self.rows - rising.shape[0]
            rising = jnp.pad(rising, ((0, rest), (0, 0)))
            falling = jnp.pad(falling, ((rest, 0), (0, 0)))
        rising, falling = add(up, rising), add(down, falling)
        if carried is not None:
            rising, falling = stack(rising, carried[0]), stack(falling, carried[1])
        self.send(rising, falling)
        self.step += 1

    def part(self, other):
        other.rising, other.falling = self.rising[self.rows:], self.falling[self.rows:]
        self.rising, self.falling = self.rising[:self.rows], self.falling[:self.rows]

    def terms(self):
        return self.packs[0][0], self.rising, self.falling


def total(ring):
    return sum(term.astype(jnp.float32) for term in ring.terms()).astype(jnp.bfloat16)


def local(patches, labels, ln_gain, w_qkv, qk_gain, w_out):
    groups = lax.axis_size("dp")
    home_packs, pack_rows = labels.shape
    spare = home_packs - WORK_P
    last = WORK_P - 1
    offsets = [1, groups // 2, groups - 1][:spare]
    me = lax.axis_index("mp").astype(jnp.int32).reshape(1)
    gain = ln_gain.reshape(1, -1)
    order = Order(labels[0, :1])

    def over_groups(values, sign, picks=(0, 1, 2)):
        return [
            lax.ppermute(
                value, "dp", [(i, (i + sign * offsets[pick]) % groups) for i in range(groups)]
            )
            for value, pick in zip(order.tie(*values), picks)
        ]

    def run(got, tags, row, slot, parts=1):
        blocks = order.tie(*got.blocks)
        sums = encode(me, tags, row, gain, qk_gain, blocks, slot, parts, w_qkv, w_out)
        order.mark(*sums)
        return sums

    def step(ring):
        ring.done()
        ring.start()

    x = Gather(order, patches[pack_rows:last * pack_rows])
    x.start()
    arrived = over_groups(pack_spare(labels, patches, WORK_P, spare), 1)
    step(x)
    order.mark(*arrived)
    rows, last_labels = merge_last(labels, patches, arrived, last)
    y = Gather(order, rows)
    y.start()
    step(x)
    step(y)
    step(x)
    y.done()
    x.done()
    y.start()
    sums1 = run(x, labels, 1, 0)
    step(y)
    sums2 = run(x, labels, 2, 1)
    y.done()
    rx = Scatter(order, sums1, sums2)
    rx.begin()
    sums3 = run(y, last_labels, 0, 1, 2)
    r3 = Scatter(order, sums3)
    rx.done()
    rx.start(sums3[7:])
    r0 = Scatter(order, run(y, labels, 0, 0, 2))
    rx.done()
    rx.part(r3)
    r3.start()
    r0.begin()
    step(r3)
    step(r0)
    rx.start()
    r3.done()
    rx.done()
    r3.start()
    step(r0)
    rx.start()
    r3.done()
    sum3 = total(r3)
    returned = over_groups([sum3] * spare, -1, (1, 0, 2))
    step(r0)
    return finish(
        labels, sums1[0], sums2[0], rx.rising, rx.falling, *r0.terms(), sum3, *returned
    )


def solution(mesh):
    placed = (P("dp", "mp"), P("dp", None), P(), P(None, None, "mp"), P(None, "mp"), P("mp", None))
    return jax.shard_map(
        local, mesh=mesh, in_specs=placed, out_specs=P("dp", "mp"), check_vma=False
    )
```

```python
import functools

import jax
import jax.numpy as jnp
from jax import lax
from jax.experimental import pallas as pl
from jax.experimental.pallas import tpu as pltpu
from jax.sharding import PartitionSpec as P

HEAD_DIM = 128
WORK_P = 4
EPSILON = 1e-06
MESH_MP = 8
VMEM_LIMIT = 52 * 1024 * 1024
SMALL_VMEM = 8 * 1024 * 1024


def normalize(values, norm_gain):
    row_mean = jnp.mean(values, axis=-1, keepdims=True)
    centered = values - row_mean
    spread = jnp.mean(centered * centered, axis=-1, keepdims=True)
    return centered * lax.rsqrt(spread + EPSILON) * norm_gain


def encode_kernel(n_mp, slot, row, me_ref, lab_ref, gain_ref, qk_ref, *refs):
    blocks, refs = refs[:9], refs[9:]
    wqkv_hbm, wout_hbm = refs[:2]
    o0, ou1, od1, ou2, od2, ou3, od3 = refs[2:9]
    far, (held, normed, wqkv, wout, sems) = refs[9:-5], refs[-5:]
    rows, width = o0.shape
    features = n_mp * width
    mine = pl.ds(slot * rows, rows)
    sources = [ref.at[mine] for ref in blocks[:7]] + [blocks[7 + slot]]
    fetches = [
        pltpu.make_async_copy(source, held.at[k], sems.at[k]) for k, source in enumerate(sources)
    ]
    loads = [
        pltpu.make_async_copy(wqkv_hbm.at[t], wqkv.at[t], sems.at[8 + t]) for t in range(3)
    ] + [pltpu.make_async_copy(wout_hbm, wout, sems.at[11])]
    for copy in fetches + loads:
        copy.start()
    me = me_ref[0]

    def columns(offset):
        return pl.ds(pl.multiple_of(lax.rem(me + offset + n_mp, n_mp) * width, width), width)

    pieces = [(held.at[k], columns(o)) for k, o in enumerate((0, -1, 1, -2, 2, -3, 3, 4))]

    def folded(part):
        return sum(part[:, c:c + 128] for c in range(0, width, 128))

    sums = jnp.zeros((rows, 128), jnp.float32)
    for (ref, _), copy in zip(pieces, fetches):
        copy.wait()
        sums = sums + folded(ref[...].astype(jnp.float32))
    mean = jnp.sum(sums, axis=1, keepdims=True) * (1.0 / features)
    sums = jnp.zeros((rows, 128), jnp.float32)
    for ref, _ in pieces:
        part = ref[...].astype(jnp.float32) - mean
        sums = sums + folded(part * part)
    spread = jnp.sum(sums, axis=1, keepdims=True) * (1.0 / features)
    scale = lax.rsqrt(spread + EPSILON)
    for ref, cols in pieces:
        part = (ref[...].astype(jnp.float32) - mean) * scale
        normed[:, cols] = (part * gain_ref[0:1, cols]).astype(jnp.bfloat16)

    projected = []
    for t in range(3):
        loads[t].wait()
        projected.append(jnp.dot(normed[...], wqkv[t], preferred_element_type=jnp.float32))
    label_row = jnp.broadcast_to(lab_ref[row:row + 1].astype(jnp.float32), (rows, rows))
    allowed = label_row == label_row.T
    attended = []
    for h in range(width // HEAD_DIM):
        cut = slice(h * HEAD_DIM, (h + 1) * HEAD_DIM)
        query = normalize(projected[0][:, cut], qk_ref[0:1, cut]).astype(jnp.bfloat16)
        key = normalize(projected[1][:, cut], qk_ref[1:2, cut]).astype(jnp.bfloat16)
        value = projected[2][:, cut].astype(jnp.bfloat16)
        score = lax.dot_general(
            query, key, (((1,), (1,)), ((), ())), preferred_element_type=jnp.float32
        ) * HEAD_DIM ** (-0.5)
        exponent = jnp.where(allowed, jnp.exp(score), 0.0)
        weight = exponent * (1.0 / jnp.sum(exponent, axis=1, keepdims=True))
        attended.append(
            jnp.dot(weight.astype(jnp.bfloat16), value, preferred_element_type=jnp.float32)
            .astype(jnp.bfloat16)
        )
    attended = jnp.concatenate(attended, axis=1)
    loads[3].wait()
    out = jnp.dot(attended, wout[:, columns(4)], preferred_element_type=jnp.float32)
    size = rows // len(far)
    for k, ref in enumerate(far):
        ref[...] = out[k * size:(k + 1) * size].astype(jnp.bfloat16)
    for ref, offset in ((ou3, 3), (od3, -3), (ou2, 2), (od2, -2), (ou1, 1), (od1, -1), (o0, 0)):
        ref[...] = jnp.dot(
            attended, wout[:, columns(offset)], preferred_element_type=jnp.float32
        ).astype(jnp.bfloat16)


def encode(me, labels, row, gain, qk_gain, blocks, slot, parts, w_qkv, w_out):
    n_mp = MESH_MP
    rows, width = blocks[0].shape[0] // 2, blocks[0].shape[1]
    features = n_mp * width
    vmem = pl.BlockSpec(memory_space=pltpu.VMEM)
    hbm = pl.BlockSpec(memory_space=pltpu.HBM)
    return pl.pallas_call(
        functools.partial(encode_kernel, n_mp, slot, row),
        out_shape=[jax.ShapeDtypeStruct((rows, width), jnp.bfloat16)] * 7
        + [jax.ShapeDtypeStruct((rows // parts, width), jnp.bfloat16)] * parts,
        in_specs=[pl.BlockSpec(memory_space=pltpu.SMEM)] + [vmem] * 3 + [hbm] * 11,
        out_specs=[vmem] * (7 + parts),
        scratch_shapes=[
            pltpu.VMEM((n_mp, rows, width), jnp.bfloat16),
            pltpu.VMEM((rows, features), jnp.bfloat16),
            pltpu.VMEM(w_qkv.shape, jnp.bfloat16),
            pltpu.VMEM(w_out.shape, jnp.bfloat16),
            pltpu.SemaphoreType.DMA((12,)),
        ],
        compiler_params=pltpu.CompilerParams(vmem_limit_bytes=VMEM_LIMIT),
        cost_estimate=pl.CostEstimate(
            flops=2 * rows * features * 4 * width,
            bytes_accessed=4 * rows * features,
            transcendentals=0,
        ),
    )(me, labels, gain, qk_gain, *blocks, w_qkv, w_out)


def pack_kernel(kept, labels_smem, labels_ref, patches_hbm, *refs):
    outs, sems = refs[:-1], refs[-1]
    pack_rows = labels_ref.shape[1]
    copies = []
    for k, out in enumerate(outs):
        rows = pl.ds((kept + k) * pack_rows, pack_rows)
        copies.append(
            pltpu.make_async_copy(patches_hbm.at[rows], out.at[pl.ds(0, pack_rows)], sems.at[k])
        )
        copies[-1].start()
    for k, out in enumerate(outs):
        tail = out.shape[0] - pack_rows
        tags = labels_ref[kept + k:kept + k + 1].astype(jnp.float32) + 1.0
        tags = jnp.broadcast_to(tags, (tail, pack_rows)).astype(jnp.bfloat16)
        out[pack_rows:, :pack_rows] = tags
        out[pack_rows:, pack_rows:] = jnp.zeros((tail, out.shape[1] - pack_rows), jnp.bfloat16)
        copies[k].wait()

        @pl.when(labels_smem[kept + k, 0] < 0)
        def _(out=out):
            out[:pack_rows] = jnp.zeros((pack_rows, out.shape[1]), jnp.bfloat16)


def pack_spare(labels, patches, kept, spare):
    pack_rows, width = labels.shape[1], patches.shape[1]
    vmem = pl.BlockSpec(memory_space=pltpu.VMEM)
    return pl.pallas_call(
        functools.partial(pack_kernel, kept),
        out_shape=[jax.ShapeDtypeStruct((pack_rows + 16, width), jnp.bfloat16)] * spare,
        in_specs=[pl.BlockSpec(memory_space=pltpu.SMEM), vmem, pl.BlockSpec(memory_space=pltpu.HBM)],
        out_specs=[vmem] * spare,
        scratch_shapes=[pltpu.SemaphoreType.DMA((spare,))],
        compiler_params=pltpu.CompilerParams(vmem_limit_bytes=SMALL_VMEM),
        cost_estimate=pl.CostEstimate(
            flops=0, bytes_accessed=4 * spare * pack_rows * width, transcendentals=0
        ),
    )(labels, labels, patches)


def merge_kernel(last, labels_smem, labels_ref, patches_hbm, a0, a1, a2, rows_ref, tags_ref, sems):
    pack_rows = labels_ref.shape[1]
    own = labels_smem[last, 0] >= 0
    head = pltpu.make_async_copy(
        patches_hbm.at[pl.ds(0, pack_rows)], rows_ref.at[pl.ds(0, pack_rows)], sems.at[0]
    )
    head.start()

    @pl.when(own)
    def _():
        source = patches_hbm.at[pl.ds(last * pack_rows, pack_rows)]
        copy = pltpu.make_async_copy(source, rows_ref.at[pl.ds(pack_rows, pack_rows)], sems.at[1])
        copy.start()
        copy.wait()
        tags_ref[...] = labels_ref[last:last + 1]

    @pl.when(jnp.logical_not(own))
    def _():
        rows_ref[pack_rows:] = a0[:pack_rows] + a1[:pack_rows] + a2[:pack_rows]
        tags = a0[pack_rows:, :pack_rows] + a1[pack_rows:, :pack_rows] + a2[pack_rows:, :pack_rows]
        tags_ref[...] = tags.astype(jnp.float32)[0:1].astype(jnp.int32) - 1

    head.wait()


def merge_last(labels, patches, arrived, last):
    pack_rows, width = labels.shape[1], patches.shape[1]
    vmem = pl.BlockSpec(memory_space=pltpu.VMEM)
    return pl.pallas_call(
        functools.partial(merge_kernel, last),
        out_shape=[
            jax.ShapeDtypeStruct((2 * pack_rows, width), jnp.bfloat16),
            jax.ShapeDtypeStruct((1, pack_rows), jnp.int32),
        ],
        in_specs=[pl.BlockSpec(memory_space=pltpu.SMEM), vmem, pl.BlockSpec(memory_space=pltpu.HBM)]
        + [vmem] * 3,
        out_specs=[vmem] * 2,
        scratch_shapes=[pltpu.SemaphoreType.DMA((2,))],
        compiler_params=pltpu.CompilerParams(vmem_limit_bytes=SMALL_VMEM),
        cost_estimate=pl.CostEstimate(
            flops=16_000_000_000, bytes_accessed=8 * pack_rows * width, transcendentals=0
        ),
    )(labels, labels, patches, *arrived)


def finish_kernel(labels_smem, x1, x2, xup, xdown, own, up, down, last, r1, r0, r2, out_hbm,
                  held, sems):
    rows = own.shape[0]
    terms = [[own, up, down]]
    for k, ref in enumerate((x1, x2)):
        cut = pl.ds(k * rows, rows)
        terms.append([ref, xup.at[cut], xdown.at[cut]])
    terms += [[last], [r0], [r1], [r2]]
    copies = []
    for pack, parts in enumerate(terms):
        values = sum(part[...].astype(jnp.float32) for part in parts)
        live = labels_smem[pack, 0] >= 0
        held[pack] = jnp.where(live, values, 0.0).astype(jnp.bfloat16)
        copies.append(
            pltpu.make_async_copy(
                held.at[pack], out_hbm.at[pl.ds(pack * rows, rows)], sems.at[pack]
            )
        )
        copies[-1].start()
    for copy in copies:
        copy.wait()


def finish(labels, *parts):
    home_packs, pack_rows = labels.shape
    width = parts[0].shape[1]
    vmem = pl.BlockSpec(memory_space=pltpu.VMEM)
    return pl.pallas_call(
        finish_kernel,
        out_shape=jax.ShapeDtypeStruct((home_packs * pack_rows, width), jnp.bfloat16),
        in_specs=[pl.BlockSpec(memory_space=pltpu.SMEM)] + [vmem] * len(parts),
        out_specs=pl.BlockSpec(memory_space=pl.ANY),
        scratch_shapes=[
            pltpu.VMEM((home_packs, pack_rows, width), jnp.bfloat16),
            pltpu.SemaphoreType.DMA((home_packs,)),
        ],
        compiler_params=pltpu.CompilerParams(vmem_limit_bytes=SMALL_VMEM),
        cost_estimate=pl.CostEstimate(
            flops=0, bytes_accessed=4 * home_packs * pack_rows * width, transcendentals=0
        ),
    )(labels, *parts)


class Order:
    def __init__(self, token):
        self.token = token

    def tie(self, *values):
        tied = lax.optimization_barrier(values + (self.token,))[:-1]
        return tied if len(tied) > 1 else tied[0]

    def mark(self, *values):
        self.token = lax.optimization_barrier((self.token,) + values)[0]


class Ring:
    def __init__(self, order):
        size = lax.axis_size("mp")
        self.order = order
        self.up = [(i, (i + 1) % size) for i in range(size)]
        self.down = [(i, (i - 1) % size) for i in range(size)]

    def send(self, rising, falling):
        rising, falling = self.order.tie(rising, falling)
        self.rising = lax.ppermute(rising, "mp", self.up)
        self.falling = lax.ppermute(falling, "mp", self.down)

    def done(self):
        self.order.mark(self.rising, self.falling)


class Gather(Ring):
    def __init__(self, order, block):
        super().__init__(order)
        self.half = block.shape[0] // 2
        self.blocks = [block]
        self.rising = self.falling = block

    def start(self):
        if len(self.blocks) < 7:
            self.send(self.rising, self.falling)
        else:
            self.send(self.rising[:self.half], self.falling[self.half:])

    def done(self):
        super().done()
        self.blocks += [self.rising, self.falling]


def add(first, second):
    return (first.astype(jnp.float32) + second.astype(jnp.float32)).astype(jnp.bfloat16)


def stack(*parts):
    return jnp.concatenate(parts, axis=0) if len(parts) > 1 else parts[0]


class Scatter(Ring):
    def __init__(self, order, *packs):
        super().__init__(order)
        self.packs = packs
        self.rows = packs[0][0].shape[0] * len(packs)
        self.step = 0

    def begin(self):
        self.send(*[part for pack in self.packs for part in pack[7:]])

    def start(self, carried=None):
        up, down = (stack(*[pack[5 - 2 * self.step + k] for pack in self.packs]) for k in range(2))
        rising, falling = self.rising, self.falling
        if self.step == 0:
            rest = self.rows - rising.shape[0]
            rising = jnp.pad(rising, ((0, rest), (0, 0)))
            falling = jnp.pad(falling, ((rest, 0), (0, 0)))
        rising, falling = add(up, rising), add(down, falling)
        if carried is not None:
            rising, falling = stack(rising, carried[0]), stack(falling, carried[1])
        self.send(rising, falling)
        self.step += 1

    def part(self, other):
        other.rising, other.falling = self.rising[self.rows:], self.falling[self.rows:]
        self.rising, self.falling = self.rising[:self.rows], self.falling[:self.rows]

    def terms(self):
        return self.packs[0][0], self.rising, self.falling


def total(ring):
    return sum(term.astype(jnp.float32) for term in ring.terms()).astype(jnp.bfloat16)


def local(patches, labels, ln_gain, w_qkv, qk_gain, w_out):
    groups = lax.axis_size("dp")
    home_packs, pack_rows = labels.shape
    spare = home_packs - WORK_P
    last = WORK_P - 1
    offsets = [1, groups // 2, groups - 1][:spare]
    me = lax.axis_index("mp").astype(jnp.int32).reshape(1)
    gain = ln_gain.reshape(1, -1)
    order = Order(labels[0, :1])

    def over_groups(values, sign, picks=(0, 1, 2)):
        return [
            lax.ppermute(
                value, "dp", [(i, (i + sign * offsets[pick]) % groups) for i in range(groups)]
            )
            for value, pick in zip(order.tie(*values), picks)
        ]

    def run(got, tags, row, slot, parts=1):
        blocks = order.tie(*got.blocks)
        sums = encode(me, tags, row, gain, qk_gain, blocks, slot, parts, w_qkv, w_out)
        order.mark(*sums)
        return sums

    def step(ring):
        ring.done()
        ring.start()

    x = Gather(order, patches[pack_rows:last * pack_rows])
    x.start()
    arrived = over_groups(pack_spare(labels, patches, WORK_P, spare), 1)
    step(x)
    order.mark(*arrived)
    rows, last_labels = merge_last(labels, patches, arrived, last)
    y = Gather(order, rows)
    y.start()
    step(x)
    y.done()
    step(x)
    x.done()
    y.start()
    sums1 = run(x, labels, 1, 0)
    step(y)
    sums2 = run(x, labels, 2, 1)
    rx = Scatter(order, sums1, sums2)
    step(y)
    rx.begin()
    y.done()
    step(rx)
    sums3 = run(y, last_labels, 0, 1, 2)
    r3 = Scatter(order, sums3)
    rx.done()
    rx.start(sums3[7:])
    r0 = Scatter(order, run(y, labels, 0, 0, 2))
    rx.done()
    rx.part(r3)
    r3.start()
    r3.done()
    r0.begin()
    r3.start()
    r3.done()
    step(r0)
    r3.start()
    step(r0)
    rx.start()
    r3.done()
    sum3 = total(r3)
    returned = over_groups([sum3] * spare, -1, (1, 0, 2))
    step(r0)
    return finish(
        labels, sums1[0], sums2[0], rx.rising, rx.falling, *r0.terms(), sum3, *returned
    )


def solution(mesh):
    placed = (P("dp", "mp"), P("dp", None), P(), P(None, None, "mp"), P(None, "mp"), P("mp", None))
    return jax.shard_map(
        local, mesh=mesh, in_specs=placed, out_specs=P("dp", "mp"), check_vma=False
    )
```

```python
import functools

import jax
import jax.numpy as jnp
from jax import lax
from jax.experimental import pallas as pl
from jax.experimental.pallas import tpu as pltpu
from jax.sharding import PartitionSpec as P

HEAD_DIM = 128
WORK_P = 4
EPSILON = 1e-06
MESH_MP = 8
VMEM_LIMIT = 52 * 1024 * 1024
SMALL_VMEM = 8 * 1024 * 1024


def normalize(values, norm_gain):
    row_mean = jnp.mean(values, axis=-1, keepdims=True)
    centered = values - row_mean
    spread = jnp.mean(centered * centered, axis=-1, keepdims=True)
    return centered * lax.rsqrt(spread + EPSILON) * norm_gain


def encode_kernel(n_mp, slot, row, me_ref, lab_ref, gain_ref, qk_ref, *refs):
    blocks, refs = refs[:9], refs[9:]
    wqkv_hbm, wout_hbm, o0, ou1, od1, ou2, od2, ou3, od3, o4, held, normed, wqkv, wout, sems = refs
    rows, width = o0.shape
    features = n_mp * width
    mine = pl.ds(slot * rows, rows)
    sources = [ref.at[mine] for ref in blocks[:7]] + [blocks[7 + slot]]
    fetches = [
        pltpu.make_async_copy(source, held.at[k], sems.at[k]) for k, source in enumerate(sources)
    ]
    loads = [
        pltpu.make_async_copy(wqkv_hbm.at[t], wqkv.at[t], sems.at[8 + t]) for t in range(3)
    ] + [pltpu.make_async_copy(wout_hbm, wout, sems.at[11])]
    for copy in fetches + loads:
        copy.start()
    me = me_ref[0]

    def columns(offset):
        return pl.ds(pl.multiple_of(lax.rem(me + offset + n_mp, n_mp) * width, width), width)

    pieces = [(held.at[k], columns(o)) for k, o in enumerate((0, -1, 1, -2, 2, -3, 3, 4))]

    def folded(part):
        return sum(part[:, c:c + 128] for c in range(0, width, 128))

    sums = jnp.zeros((rows, 128), jnp.float32)
    for (ref, _), copy in zip(pieces, fetches):
        copy.wait()
        sums = sums + folded(ref[...].astype(jnp.float32))
    mean = jnp.sum(sums, axis=1, keepdims=True) * (1.0 / features)
    sums = jnp.zeros((rows, 128), jnp.float32)
    for ref, _ in pieces:
        part = ref[...].astype(jnp.float32) - mean
        sums = sums + folded(part * part)
    spread = jnp.sum(sums, axis=1, keepdims=True) * (1.0 / features)
    scale = lax.rsqrt(spread + EPSILON)
    for ref, cols in pieces:
        part = (ref[...].astype(jnp.float32) - mean) * scale
        normed[:, cols] = (part * gain_ref[0:1, cols]).astype(jnp.bfloat16)

    projected = []
    for t in range(3):
        loads[t].wait()
        projected.append(jnp.dot(normed[...], wqkv[t], preferred_element_type=jnp.float32))
    label_row = jnp.broadcast_to(lab_ref[row:row + 1].astype(jnp.float32), (rows, rows))
    allowed = label_row == label_row.T
    attended = []
    for h in range(width // HEAD_DIM):
        cut = slice(h * HEAD_DIM, (h + 1) * HEAD_DIM)
        query = normalize(projected[0][:, cut], qk_ref[0:1, cut]).astype(jnp.bfloat16)
        key = normalize(projected[1][:, cut], qk_ref[1:2, cut]).astype(jnp.bfloat16)
        value = projected[2][:, cut].astype(jnp.bfloat16)
        score = lax.dot_general(
            query, key, (((1,), (1,)), ((), ())), preferred_element_type=jnp.float32
        ) * HEAD_DIM ** (-0.5)
        exponent = jnp.where(allowed, jnp.exp(score), 0.0)
        weight = exponent * (1.0 / jnp.sum(exponent, axis=1, keepdims=True))
        attended.append(
            jnp.dot(weight.astype(jnp.bfloat16), value, preferred_element_type=jnp.float32)
            .astype(jnp.bfloat16)
        )
    attended = jnp.concatenate(attended, axis=1)
    loads[3].wait()
    for ref, offset in ((o4, 4), (ou3, 3), (od3, -3), (ou2, 2), (od2, -2), (ou1, 1), (od1, -1), (o0, 0)):
        ref[...] = jnp.dot(
            attended, wout[:, columns(offset)], preferred_element_type=jnp.float32
        ).astype(jnp.bfloat16)


def encode(me, labels, row, gain, qk_gain, blocks, slot, w_qkv, w_out):
    n_mp = MESH_MP
    rows, width = blocks[0].shape[0] // 2, blocks[0].shape[1]
    features = n_mp * width
    vmem = pl.BlockSpec(memory_space=pltpu.VMEM)
    hbm = pl.BlockSpec(memory_space=pltpu.HBM)
    return pl.pallas_call(
        functools.partial(encode_kernel, n_mp, slot, row),
        out_shape=[jax.ShapeDtypeStruct((rows, width), jnp.bfloat16)] * 8,
        in_specs=[pl.BlockSpec(memory_space=pltpu.SMEM)] + [vmem] * 3 + [hbm] * 11,
        out_specs=[vmem] * 8,
        scratch_shapes=[
            pltpu.VMEM((n_mp, rows, width), jnp.bfloat16),
            pltpu.VMEM((rows, features), jnp.bfloat16),
            pltpu.VMEM(w_qkv.shape, jnp.bfloat16),
            pltpu.VMEM(w_out.shape, jnp.bfloat16),
            pltpu.SemaphoreType.DMA((12,)),
        ],
        compiler_params=pltpu.CompilerParams(vmem_limit_bytes=VMEM_LIMIT),
        cost_estimate=pl.CostEstimate(
            flops=2 * rows * features * 4 * width,
            bytes_accessed=4 * rows * features,
            transcendentals=0,
        ),
    )(me, labels, gain, qk_gain, *blocks, w_qkv, w_out)


def pack_kernel(kept, labels_smem, labels_ref, patches_hbm, *refs):
    outs, sems = refs[:-1], refs[-1]
    pack_rows = labels_ref.shape[1]
    copies = []
    for k, out in enumerate(outs):
        rows = pl.ds((kept + k) * pack_rows, pack_rows)
        copies.append(
            pltpu.make_async_copy(patches_hbm.at[rows], out.at[pl.ds(0, pack_rows)], sems.at[k])
        )
        copies[-1].start()
    for k, out in enumerate(outs):
        tail = out.shape[0] - pack_rows
        tags = labels_ref[kept + k:kept + k + 1].astype(jnp.float32) + 1.0
        tags = jnp.broadcast_to(tags, (tail, pack_rows)).astype(jnp.bfloat16)
        out[pack_rows:, :pack_rows] = tags
        out[pack_rows:, pack_rows:] = jnp.zeros((tail, out.shape[1] - pack_rows), jnp.bfloat16)
        copies[k].wait()

        @pl.when(labels_smem[kept + k, 0] < 0)
        def _(out=out):
            out[:pack_rows] = jnp.zeros((pack_rows, out.shape[1]), jnp.bfloat16)


def pack_spare(labels, patches, kept, spare):
    pack_rows, width = labels.shape[1], patches.shape[1]
    vmem = pl.BlockSpec(memory_space=pltpu.VMEM)
    return pl.pallas_call(
        functools.partial(pack_kernel, kept),
        out_shape=[jax.ShapeDtypeStruct((pack_rows + 16, width), jnp.bfloat16)] * spare,
        in_specs=[pl.BlockSpec(memory_space=pltpu.SMEM), vmem, pl.BlockSpec(memory_space=pltpu.HBM)],
        out_specs=[vmem] * spare,
        scratch_shapes=[pltpu.SemaphoreType.DMA((spare,))],
        compiler_params=pltpu.CompilerParams(vmem_limit_bytes=SMALL_VMEM),
        cost_estimate=pl.CostEstimate(
            flops=0, bytes_accessed=4 * spare * pack_rows * width, transcendentals=0
        ),
    )(labels, labels, patches)


def merge_kernel(last, labels_smem, labels_ref, patches_hbm, a0, a1, a2, rows_ref, tags_ref, sems):
    pack_rows = labels_ref.shape[1]
    own = labels_smem[last, 0] >= 0
    head = pltpu.make_async_copy(
        patches_hbm.at[pl.ds(0, pack_rows)], rows_ref.at[pl.ds(0, pack_rows)], sems.at[0]
    )
    head.start()

    @pl.when(own)
    def _():
        source = patches_hbm.at[pl.ds(last * pack_rows, pack_rows)]
        copy = pltpu.make_async_copy(source, rows_ref.at[pl.ds(pack_rows, pack_rows)], sems.at[1])
        copy.start()
        copy.wait()
        tags_ref[...] = labels_ref[last:last + 1]

    @pl.when(jnp.logical_not(own))
    def _():
        rows_ref[pack_rows:] = a0[:pack_rows] + a1[:pack_rows] + a2[:pack_rows]
        tags = a0[pack_rows:, :pack_rows] + a1[pack_rows:, :pack_rows] + a2[pack_rows:, :pack_rows]
        tags_ref[...] = tags.astype(jnp.float32)[0:1].astype(jnp.int32) - 1

    head.wait()


def merge_last(labels, patches, arrived, last):
    pack_rows, width = labels.shape[1], patches.shape[1]
    vmem = pl.BlockSpec(memory_space=pltpu.VMEM)
    return pl.pallas_call(
        functools.partial(merge_kernel, last),
        out_shape=[
            jax.ShapeDtypeStruct((2 * pack_rows, width), jnp.bfloat16),
            jax.ShapeDtypeStruct((1, pack_rows), jnp.int32),
        ],
        in_specs=[pl.BlockSpec(memory_space=pltpu.SMEM), vmem, pl.BlockSpec(memory_space=pltpu.HBM)]
        + [vmem] * 3,
        out_specs=[vmem] * 2,
        scratch_shapes=[pltpu.SemaphoreType.DMA((2,))],
        compiler_params=pltpu.CompilerParams(vmem_limit_bytes=SMALL_VMEM),
        cost_estimate=pl.CostEstimate(
            flops=16_000_000_000, bytes_accessed=8 * pack_rows * width, transcendentals=0
        ),
    )(labels, labels, patches, *arrived)


def finish_kernel(labels_smem, x1, x2, xup, xdown, own, up, down, last, r1, r0, r2, out_hbm,
                  held, sems):
    rows = own.shape[0]
    terms = [[own, up, down]]
    for k, ref in enumerate((x1, x2)):
        cut = pl.ds(k * rows, rows)
        terms.append([ref, xup.at[cut], xdown.at[cut]])
    terms += [[last], [r0], [r1], [r2]]
    copies = []
    for pack, parts in enumerate(terms):
        values = sum(part[...].astype(jnp.float32) for part in parts)
        live = labels_smem[pack, 0] >= 0
        held[pack] = jnp.where(live, values, 0.0).astype(jnp.bfloat16)
        copies.append(
            pltpu.make_async_copy(
                held.at[pack], out_hbm.at[pl.ds(pack * rows, rows)], sems.at[pack]
            )
        )
        copies[-1].start()
    for copy in copies:
        copy.wait()


def finish(labels, *parts):
    home_packs, pack_rows = labels.shape
    width = parts[0].shape[1]
    vmem = pl.BlockSpec(memory_space=pltpu.VMEM)
    return pl.pallas_call(
        finish_kernel,
        out_shape=jax.ShapeDtypeStruct((home_packs * pack_rows, width), jnp.bfloat16),
        in_specs=[pl.BlockSpec(memory_space=pltpu.SMEM)] + [vmem] * len(parts),
        out_specs=pl.BlockSpec(memory_space=pl.ANY),
        scratch_shapes=[
            pltpu.VMEM((home_packs, pack_rows, width), jnp.bfloat16),
            pltpu.SemaphoreType.DMA((home_packs,)),
        ],
        compiler_params=pltpu.CompilerParams(vmem_limit_bytes=SMALL_VMEM),
        cost_estimate=pl.CostEstimate(
            flops=0, bytes_accessed=4 * home_packs * pack_rows * width, transcendentals=0
        ),
    )(labels, *parts)


class Order:
    def __init__(self, token):
        self.token = token

    def tie(self, *values):
        tied = lax.optimization_barrier(values + (self.token,))[:-1]
        return tied if len(tied) > 1 else tied[0]

    def mark(self, *values):
        self.token = lax.optimization_barrier((self.token,) + values)[0]


class Ring:
    def __init__(self, order):
        size = lax.axis_size("mp")
        self.order = order
        self.up = [(i, (i + 1) % size) for i in range(size)]
        self.down = [(i, (i - 1) % size) for i in range(size)]

    def send(self, rising, falling):
        rising, falling = self.order.tie(rising, falling)
        self.rising = lax.ppermute(rising, "mp", self.up)
        self.falling = lax.ppermute(falling, "mp", self.down)

    def done(self):
        self.order.mark(self.rising, self.falling)


class Gather(Ring):
    def __init__(self, order, block):
        super().__init__(order)
        self.half = block.shape[0] // 2
        self.blocks = [block]
        self.rising = self.falling = block

    def start(self):
        if len(self.blocks) < 7:
            self.send(self.rising, self.falling)
        else:
            self.send(self.rising[:self.half], self.falling[self.half:])

    def done(self):
        super().done()
        self.blocks += [self.rising, self.falling]


def add(first, second):
    return (first.astype(jnp.float32) + second.astype(jnp.float32)).astype(jnp.bfloat16)


def stack(parts):
    return jnp.concatenate(parts, axis=0) if len(parts) > 1 else parts[0]


class Scatter(Ring):
    def __init__(self, order, *packs):
        super().__init__(order)
        self.packs = packs
        self.step = 0

    def begin(self):
        self.send(self.packs[0][7], self.packs[1][7])

    def apart(self):
        chains = [Scatter(self.order, pack) for pack in self.packs]
        chains[0].rising, chains[0].falling = self.rising, None
        chains[1].rising, chains[1].falling = None, self.falling
        return chains

    def start(self):
        up, down = ([pack[5 - 2 * self.step + k] for pack in self.packs] for k in range(2))
        if len(self.packs) == 2 and self.step == 0:
            up[0], down[1] = add(up[0], self.rising), add(down[1], self.falling)
            self.send(stack(up), stack(down))
        else:
            rising, falling = stack(up), stack(down)
            self.send(
                rising if self.rising is None else add(rising, self.rising),
                falling if self.falling is None else add(falling, self.falling),
            )
        self.step += 1

    def terms(self):
        return self.packs[0][0], self.rising, self.falling


def total(ring):
    return sum(term.astype(jnp.float32) for term in ring.terms()).astype(jnp.bfloat16)


def local(patches, labels, ln_gain, w_qkv, qk_gain, w_out):
    groups = lax.axis_size("dp")
    home_packs, pack_rows = labels.shape
    spare = home_packs - WORK_P
    last = WORK_P - 1
    offsets = [1, groups // 2, groups - 1][:spare]
    me = lax.axis_index("mp").astype(jnp.int32).reshape(1)
    gain = ln_gain.reshape(1, -1)
    order = Order(labels[0, :1])

    def over_groups(values, sign, picks=(0, 1, 2)):
        return [
            lax.ppermute(
                value, "dp", [(i, (i + sign * offsets[pick]) % groups) for i in range(groups)]
            )
            for value, pick in zip(order.tie(*values), picks)
        ]

    def run(got, tags, row, slot):
        sums = encode(me, tags, row, gain, qk_gain, order.tie(*got.blocks), slot, w_qkv, w_out)
        order.mark(*sums)
        return sums

    def step(ring):
        ring.done()
        ring.start()

    x = Gather(order, patches[pack_rows:last * pack_rows])
    x.start()
    arrived = over_groups(pack_spare(labels, patches, WORK_P, spare), 1)
    step(x)
    order.mark(*arrived)
    rows, last_labels = merge_last(labels, patches, arrived, last)
    y = Gather(order, rows)
    y.start()
    step(x)
    y.done()
    step(x)
    x.done()
    y.start()
    sums1 = run(x, labels, 1, 0)
    step(y)
    sums2 = run(x, labels, 2, 1)
    rx = Scatter(order, sums1, sums2)
    step(y)
    rx.begin()
    y.done()
    step(rx)
    sums3 = run(y, last_labels, 0, 1)
    step(rx)
    sums0 = run(y, labels, 0, 0)
    rx.done()
    ry = Scatter(order, sums0, sums3)
    ry.begin()
    ry.done()
    r0, r3 = ry.apart()
    r3.start()
    r0.start()
    step(r3)
    step(r0)
    step(r3)
    rx.start()
    r3.done()
    sum3 = total(r3)
    returned = over_groups([sum3] * spare, -1, (1, 0, 2))
    step(r0)
    return finish(
        labels, sums1[0], sums2[0], rx.rising, rx.falling, *r0.terms(), sum3, *returned
    )


def solution(mesh):
    placed = (P("dp", "mp"), P("dp", None), P(), P(None, None, "mp"), P(None, "mp"), P("mp", None))
    return jax.shard_map(
        local, mesh=mesh, in_specs=placed, out_specs=P("dp", "mp"), check_vma=False
    )
```

```python
import functools

import jax
import jax.numpy as jnp
from jax import lax
from jax.experimental import pallas as pl
from jax.experimental.pallas import tpu as pltpu
from jax.sharding import PartitionSpec as P

HEAD_DIM = 128
WORK_P = 4
EPSILON = 1e-06
MESH_MP = 8
VMEM_LIMIT = 52 * 1024 * 1024
SMALL_VMEM = 8 * 1024 * 1024


def normalize(values, norm_gain):
    row_mean = jnp.mean(values, axis=-1, keepdims=True)
    centered = values - row_mean
    spread = jnp.mean(centered * centered, axis=-1, keepdims=True)
    return centered * lax.rsqrt(spread + EPSILON) * norm_gain


def encode_kernel(n_mp, slot, row, me_ref, lab_ref, gain_ref, qk_ref, *refs):
    blocks, refs = refs[:9], refs[9:]
    wqkv_hbm, wout_hbm, o0, ou1, od1, ou2, od2, ou3, od3, o4, held, normed, wqkv, wout, sems = refs
    rows, width = o0.shape
    features = n_mp * width
    mine = pl.ds(slot * rows, rows)
    sources = [ref.at[mine] for ref in blocks[:7]] + [blocks[7 + slot]]
    fetches = [
        pltpu.make_async_copy(source, held.at[k], sems.at[k]) for k, source in enumerate(sources)
    ]
    loads = [
        pltpu.make_async_copy(wqkv_hbm.at[t], wqkv.at[t], sems.at[8 + t]) for t in range(3)
    ] + [pltpu.make_async_copy(wout_hbm, wout, sems.at[11])]
    for copy in fetches + loads:
        copy.start()
    me = me_ref[0]

    def columns(offset):
        return pl.ds(pl.multiple_of(lax.rem(me + offset + n_mp, n_mp) * width, width), width)

    pieces = [(held.at[k], columns(o)) for k, o in enumerate((0, -1, 1, -2, 2, -3, 3, 4))]

    def folded(part):
        return sum(part[:, c:c + 128] for c in range(0, width, 128))

    sums = jnp.zeros((rows, 128), jnp.float32)
    for (ref, _), copy in zip(pieces, fetches):
        copy.wait()
        sums = sums + folded(ref[...].astype(jnp.float32))
    mean = jnp.sum(sums, axis=1, keepdims=True) * (1.0 / features)
    sums = jnp.zeros((rows, 128), jnp.float32)
    for ref, _ in pieces:
        part = ref[...].astype(jnp.float32) - mean
        sums = sums + folded(part * part)
    spread = jnp.sum(sums, axis=1, keepdims=True) * (1.0 / features)
    scale = lax.rsqrt(spread + EPSILON)
    for ref, cols in pieces:
        part = (ref[...].astype(jnp.float32) - mean) * scale
        normed[:, cols] = (part * gain_ref[0:1, cols]).astype(jnp.bfloat16)

    projected = []
    for t in range(3):
        loads[t].wait()
        projected.append(jnp.dot(normed[...], wqkv[t], preferred_element_type=jnp.float32))
    label_row = jnp.broadcast_to(lab_ref[row:row + 1].astype(jnp.float32), (rows, rows))
    allowed = label_row == label_row.T
    attended = []
    for h in range(width // HEAD_DIM):
        cut = slice(h * HEAD_DIM, (h + 1) * HEAD_DIM)
        query = normalize(projected[0][:, cut], qk_ref[0:1, cut]).astype(jnp.bfloat16)
        key = normalize(projected[1][:, cut], qk_ref[1:2, cut]).astype(jnp.bfloat16)
        value = projected[2][:, cut].astype(jnp.bfloat16)
        score = lax.dot_general(
            query, key, (((1,), (1,)), ((), ())), preferred_element_type=jnp.float32
        ) * HEAD_DIM ** (-0.5)
        exponent = jnp.where(allowed, jnp.exp(score), 0.0)
        weight = exponent * (1.0 / jnp.sum(exponent, axis=1, keepdims=True))
        attended.append(
            jnp.dot(weight.astype(jnp.bfloat16), value, preferred_element_type=jnp.float32)
            .astype(jnp.bfloat16)
        )
    attended = jnp.concatenate(attended, axis=1)
    loads[3].wait()
    for ref, offset in ((o4, 4), (ou3, 3), (od3, -3), (ou2, 2), (od2, -2), (ou1, 1), (od1, -1), (o0, 0)):
        ref[...] = jnp.dot(
            attended, wout[:, columns(offset)], preferred_element_type=jnp.float32
        ).astype(jnp.bfloat16)


def encode(me, labels, row, gain, qk_gain, blocks, slot, w_qkv, w_out):
    n_mp = MESH_MP
    rows, width = blocks[0].shape[0] // 2, blocks[0].shape[1]
    features = n_mp * width
    vmem = pl.BlockSpec(memory_space=pltpu.VMEM)
    hbm = pl.BlockSpec(memory_space=pltpu.HBM)
    return pl.pallas_call(
        functools.partial(encode_kernel, n_mp, slot, row),
        out_shape=[jax.ShapeDtypeStruct((rows, width), jnp.bfloat16)] * 8,
        in_specs=[pl.BlockSpec(memory_space=pltpu.SMEM)] + [vmem] * 3 + [hbm] * 11,
        out_specs=[vmem] * 8,
        scratch_shapes=[
            pltpu.VMEM((n_mp, rows, width), jnp.bfloat16),
            pltpu.VMEM((rows, features), jnp.bfloat16),
            pltpu.VMEM(w_qkv.shape, jnp.bfloat16),
            pltpu.VMEM(w_out.shape, jnp.bfloat16),
            pltpu.SemaphoreType.DMA((12,)),
        ],
        compiler_params=pltpu.CompilerParams(vmem_limit_bytes=VMEM_LIMIT),
        cost_estimate=pl.CostEstimate(
            flops=2 * rows * features * 4 * width,
            bytes_accessed=4 * rows * features,
            transcendentals=0,
        ),
    )(me, labels, gain, qk_gain, *blocks, w_qkv, w_out)


def pack_kernel(kept, labels_smem, labels_ref, patches_hbm, *refs):
    outs, sems = refs[:-1], refs[-1]
    pack_rows = labels_ref.shape[1]
    copies = []
    for k, out in enumerate(outs):
        rows = pl.ds((kept + k) * pack_rows, pack_rows)
        copies.append(
            pltpu.make_async_copy(patches_hbm.at[rows], out.at[pl.ds(0, pack_rows)], sems.at[k])
        )
        copies[-1].start()
    for k, out in enumerate(outs):
        tail = out.shape[0] - pack_rows
        tags = labels_ref[kept + k:kept + k + 1].astype(jnp.float32) + 1.0
        tags = jnp.broadcast_to(tags, (tail, pack_rows)).astype(jnp.bfloat16)
        out[pack_rows:, :pack_rows] = tags
        out[pack_rows:, pack_rows:] = jnp.zeros((tail, out.shape[1] - pack_rows), jnp.bfloat16)
        copies[k].wait()

        @pl.when(labels_smem[kept + k, 0] < 0)
        def _(out=out):
            out[:pack_rows] = jnp.zeros((pack_rows, out.shape[1]), jnp.bfloat16)


def pack_spare(labels, patches, kept, spare):
    pack_rows, width = labels.shape[1], patches.shape[1]
    vmem = pl.BlockSpec(memory_space=pltpu.VMEM)
    return pl.pallas_call(
        functools.partial(pack_kernel, kept),
        out_shape=[jax.ShapeDtypeStruct((pack_rows + 16, width), jnp.bfloat16)] * spare,
        in_specs=[pl.BlockSpec(memory_space=pltpu.SMEM), vmem, pl.BlockSpec(memory_space=pltpu.HBM)],
        out_specs=[vmem] * spare,
        scratch_shapes=[pltpu.SemaphoreType.DMA((spare,))],
        compiler_params=pltpu.CompilerParams(vmem_limit_bytes=SMALL_VMEM),
        cost_estimate=pl.CostEstimate(
            flops=0, bytes_accessed=4 * spare * pack_rows * width, transcendentals=0
        ),
    )(labels, labels, patches)


def merge_kernel(last, labels_smem, labels_ref, patches_hbm, a0, a1, a2, rows_ref, tags_ref, sems):
    pack_rows = labels_ref.shape[1]
    own = labels_smem[last, 0] >= 0
    head = pltpu.make_async_copy(
        patches_hbm.at[pl.ds(0, pack_rows)], rows_ref.at[pl.ds(0, pack_rows)], sems.at[0]
    )
    head.start()

    @pl.when(own)
    def _():
        source = patches_hbm.at[pl.ds(last * pack_rows, pack_rows)]
        copy = pltpu.make_async_copy(source, rows_ref.at[pl.ds(pack_rows, pack_rows)], sems.at[1])
        copy.start()
        copy.wait()
        tags_ref[...] = labels_ref[last:last + 1]

    @pl.when(jnp.logical_not(own))
    def _():
        rows_ref[pack_rows:] = a0[:pack_rows] + a1[:pack_rows] + a2[:pack_rows]
        tags = a0[pack_rows:, :pack_rows] + a1[pack_rows:, :pack_rows] + a2[pack_rows:, :pack_rows]
        tags_ref[...] = tags.astype(jnp.float32)[0:1].astype(jnp.int32) - 1

    head.wait()


def merge_last(labels, patches, arrived, last):
    pack_rows, width = labels.shape[1], patches.shape[1]
    vmem = pl.BlockSpec(memory_space=pltpu.VMEM)
    return pl.pallas_call(
        functools.partial(merge_kernel, last),
        out_shape=[
            jax.ShapeDtypeStruct((2 * pack_rows, width), jnp.bfloat16),
            jax.ShapeDtypeStruct((1, pack_rows), jnp.int32),
        ],
        in_specs=[pl.BlockSpec(memory_space=pltpu.SMEM), vmem, pl.BlockSpec(memory_space=pltpu.HBM)]
        + [vmem] * 3,
        out_specs=[vmem] * 2,
        scratch_shapes=[pltpu.SemaphoreType.DMA((2,))],
        compiler_params=pltpu.CompilerParams(vmem_limit_bytes=SMALL_VMEM),
        cost_estimate=pl.CostEstimate(
            flops=16_000_000_000, bytes_accessed=8 * pack_rows * width, transcendentals=0
        ),
    )(labels, labels, patches, *arrived)


def finish_kernel(labels_smem, x1, x2, xup, xdown, own, up, down, last, r1, r0, r2, out_hbm,
                  held, sems):
    rows = own.shape[0]
    terms = [[own, up, down]]
    for k, ref in enumerate((x1, x2)):
        cut = pl.ds(k * rows, rows)
        terms.append([ref, xup.at[cut], xdown.at[cut]])
    terms += [[last], [r0], [r1], [r2]]
    copies = []
    for pack, parts in enumerate(terms):
        values = sum(part[...].astype(jnp.float32) for part in parts)
        live = labels_smem[pack, 0] >= 0
        held[pack] = jnp.where(live, values, 0.0).astype(jnp.bfloat16)
        copies.append(
            pltpu.make_async_copy(
                held.at[pack], out_hbm.at[pl.ds(pack * rows, rows)], sems.at[pack]
            )
        )
        copies[-1].start()
    for copy in copies:
        copy.wait()


def finish(labels, *parts):
    home_packs, pack_rows = labels.shape
    width = parts[0].shape[1]
    vmem = pl.BlockSpec(memory_space=pltpu.VMEM)
    return pl.pallas_call(
        finish_kernel,
        out_shape=jax.ShapeDtypeStruct((home_packs * pack_rows, width), jnp.bfloat16),
        in_specs=[pl.BlockSpec(memory_space=pltpu.SMEM)] + [vmem] * len(parts),
        out_specs=pl.BlockSpec(memory_space=pl.ANY),
        scratch_shapes=[
            pltpu.VMEM((home_packs, pack_rows, width), jnp.bfloat16),
            pltpu.SemaphoreType.DMA((home_packs,)),
        ],
        compiler_params=pltpu.CompilerParams(vmem_limit_bytes=SMALL_VMEM),
        cost_estimate=pl.CostEstimate(
            flops=0, bytes_accessed=4 * home_packs * pack_rows * width, transcendentals=0
        ),
    )(labels, *parts)


class Order:
    def __init__(self, token):
        self.token = token

    def tie(self, *values):
        tied = lax.optimization_barrier(values + (self.token,))[:-1]
        return tied if len(tied) > 1 else tied[0]

    def mark(self, *values):
        self.token = lax.optimization_barrier((self.token,) + values)[0]


class Ring:
    def __init__(self, order):
        size = lax.axis_size("mp")
        self.order = order
        self.up = [(i, (i + 1) % size) for i in range(size)]
        self.down = [(i, (i - 1) % size) for i in range(size)]

    def send(self, rising, falling):
        rising, falling = self.order.tie(rising, falling)
        self.rising = lax.ppermute(rising, "mp", self.up)
        self.falling = lax.ppermute(falling, "mp", self.down)

    def done(self):
        self.order.mark(self.rising, self.falling)


class Gather(Ring):
    def __init__(self, order, block):
        super().__init__(order)
        self.half = block.shape[0] // 2
        self.blocks = [block]
        self.rising = self.falling = block

    def start(self):
        if len(self.blocks) < 7:
            self.send(self.rising, self.falling)
        else:
            self.send(self.rising[:self.half], self.falling[self.half:])

    def done(self):
        super().done()
        self.blocks += [self.rising, self.falling]


def add(first, second):
    return (first.astype(jnp.float32) + second.astype(jnp.float32)).astype(jnp.bfloat16)


def stack(parts):
    return jnp.concatenate(parts, axis=0) if len(parts) > 1 else parts[0]


class Scatter(Ring):
    def __init__(self, order, *packs):
        super().__init__(order)
        self.packs = packs
        self.step = 0

    def begin(self):
        self.send(self.packs[0][7], self.packs[1][7])

    def apart(self):
        chains = [Scatter(self.order, pack) for pack in self.packs]
        chains[0].rising, chains[0].falling = self.rising, None
        chains[1].rising, chains[1].falling = None, self.falling
        return chains

    def start(self):
        up, down = ([pack[5 - 2 * self.step + k] for pack in self.packs] for k in range(2))
        if len(self.packs) == 2 and self.step == 0:
            up[0], down[1] = add(up[0], self.rising), add(down[1], self.falling)
            self.send(stack(up), stack(down))
        else:
            rising, falling = stack(up), stack(down)
            self.send(
                rising if self.rising is None else add(rising, self.rising),
                falling if self.falling is None else add(falling, self.falling),
            )
        self.step += 1

    def terms(self):
        return self.packs[0][0], self.rising, self.falling


def total(ring):
    return sum(term.astype(jnp.float32) for term in ring.terms()).astype(jnp.bfloat16)


def local(patches, labels, ln_gain, w_qkv, qk_gain, w_out):
    groups = lax.axis_size("dp")
    home_packs, pack_rows = labels.shape
    spare = home_packs - WORK_P
    last = WORK_P - 1
    offsets = [1, groups // 2, groups - 1][:spare]
    me = lax.axis_index("mp").astype(jnp.int32).reshape(1)
    gain = ln_gain.reshape(1, -1)
    order = Order(labels[0, :1])

    def over_groups(values, sign, picks=(0, 1, 2)):
        return [
            lax.ppermute(
                value, "dp", [(i, (i + sign * offsets[pick]) % groups) for i in range(groups)]
            )
            for value, pick in zip(order.tie(*values), picks)
        ]

    def run(got, tags, row, slot):
        sums = encode(me, tags, row, gain, qk_gain, order.tie(*got.blocks), slot, w_qkv, w_out)
        order.mark(*sums)
        return sums

    def step(ring):
        ring.done()
        ring.start()

    x = Gather(order, patches[pack_rows:last * pack_rows])
    x.start()
    arrived = over_groups(pack_spare(labels, patches, WORK_P, spare), 1)
    step(x)
    order.mark(*arrived)
    rows, last_labels = merge_last(labels, patches, arrived, last)
    y = Gather(order, rows)
    y.start()
    step(x)
    y.done()
    step(x)
    x.done()
    y.start()
    sums1 = run(x, labels, 1, 0)
    step(y)
    sums2 = run(x, labels, 2, 1)
    rx = Scatter(order, sums1, sums2)
    step(y)
    rx.begin()
    y.done()
    step(rx)
    sums3 = run(y, last_labels, 0, 1)
    step(rx)
    sums0 = run(y, labels, 0, 0)
    rx.done()
    ry = Scatter(order, sums0, sums3)
    ry.begin()
    rx.start()
    ry.done()
    r0, r3 = ry.apart()
    r3.start()
    rx.done()
    r0.start()
    step(r3)
    step(r0)
    step(r3)
    r3.done()
    sum3 = total(r3)
    returned = over_groups([sum3] * spare, -1, (1, 0, 2))
    step(r0)
    return finish(
        labels, sums1[0], sums2[0], rx.rising, rx.falling, *r0.terms(), sum3, *returned
    )


def solution(mesh):
    placed = (P("dp", "mp"), P("dp", None), P(), P(None, None, "mp"), P(None, "mp"), P("mp", None))
    return jax.shard_map(
        local, mesh=mesh, in_specs=placed, out_specs=P("dp", "mp"), check_vma=False
    )
```

```python
import functools

import jax
import jax.numpy as jnp
from jax import lax
from jax.experimental import pallas as pl
from jax.experimental.pallas import tpu as pltpu
from jax.sharding import PartitionSpec as P

HEAD_DIM = 128
WORK_P = 4
EPSILON = 1e-06
MESH_MP = 8
VMEM_LIMIT = 52 * 1024 * 1024
SMALL_VMEM = 8 * 1024 * 1024


def normalize(values, norm_gain):
    row_mean = jnp.mean(values, axis=-1, keepdims=True)
    centered = values - row_mean
    spread = jnp.mean(centered * centered, axis=-1, keepdims=True)
    return centered * lax.rsqrt(spread + EPSILON) * norm_gain


def encode_kernel(n_mp, slot, row, me_ref, lab_ref, gain_ref, qk_ref, *refs):
    blocks, refs = refs[:9], refs[9:]
    wqkv_hbm, wout_hbm, o0, ou1, od1, ou2, od2, ou3, od3, o4, held, normed, wqkv, wout, sems = refs
    rows, width = o0.shape
    features = n_mp * width
    mine = pl.ds(slot * rows, rows)
    sources = [ref.at[mine] for ref in blocks[:7]] + [blocks[7 + slot]]
    fetches = [
        pltpu.make_async_copy(source, held.at[k], sems.at[k]) for k, source in enumerate(sources)
    ]
    loads = [
        pltpu.make_async_copy(wqkv_hbm.at[t], wqkv.at[t], sems.at[8 + t]) for t in range(3)
    ] + [pltpu.make_async_copy(wout_hbm, wout, sems.at[11])]
    for copy in fetches + loads:
        copy.start()
    me = me_ref[0]

    def columns(offset):
        return pl.ds(pl.multiple_of(lax.rem(me + offset + n_mp, n_mp) * width, width), width)

    pieces = [(held.at[k], columns(o)) for k, o in enumerate((0, -1, 1, -2, 2, -3, 3, 4))]

    def folded(part):
        return sum(part[:, c:c + 128] for c in range(0, width, 128))

    sums = jnp.zeros((rows, 128), jnp.float32)
    for (ref, _), copy in zip(pieces, fetches):
        copy.wait()
        sums = sums + folded(ref[...].astype(jnp.float32))
    mean = jnp.sum(sums, axis=1, keepdims=True) * (1.0 / features)
    sums = jnp.zeros((rows, 128), jnp.float32)
    for ref, _ in pieces:
        part = ref[...].astype(jnp.float32) - mean
        sums = sums + folded(part * part)
    spread = jnp.sum(sums, axis=1, keepdims=True) * (1.0 / features)
    scale = lax.rsqrt(spread + EPSILON)
    for ref, cols in pieces:
        part = (ref[...].astype(jnp.float32) - mean) * scale
        normed[:, cols] = (part * gain_ref[0:1, cols]).astype(jnp.bfloat16)

    projected = []
    for t in range(3):
        loads[t].wait()
        projected.append(jnp.dot(normed[...], wqkv[t], preferred_element_type=jnp.float32))
    label_row = jnp.broadcast_to(lab_ref[row:row + 1].astype(jnp.float32), (rows, rows))
    allowed = label_row == label_row.T
    attended = []
    for h in range(width // HEAD_DIM):
        cut = slice(h * HEAD_DIM, (h + 1) * HEAD_DIM)
        query = normalize(projected[0][:, cut], qk_ref[0:1, cut]).astype(jnp.bfloat16)
        key = normalize(projected[1][:, cut], qk_ref[1:2, cut]).astype(jnp.bfloat16)
        value = projected[2][:, cut].astype(jnp.bfloat16)
        score = lax.dot_general(
            query, key, (((1,), (1,)), ((), ())), preferred_element_type=jnp.float32
        ) * HEAD_DIM ** (-0.5)
        exponent = jnp.where(allowed, jnp.exp(score), 0.0)
        weight = exponent * (1.0 / jnp.sum(exponent, axis=1, keepdims=True))
        attended.append(
            jnp.dot(weight.astype(jnp.bfloat16), value, preferred_element_type=jnp.float32)
            .astype(jnp.bfloat16)
        )
    attended = jnp.concatenate(attended, axis=1)
    loads[3].wait()
    for ref, offset in ((o4, 4), (ou3, 3), (od3, -3), (ou2, 2), (od2, -2), (ou1, 1), (od1, -1), (o0, 0)):
        ref[...] = jnp.dot(
            attended, wout[:, columns(offset)], preferred_element_type=jnp.float32
        ).astype(jnp.bfloat16)


def encode(me, labels, row, gain, qk_gain, blocks, slot, w_qkv, w_out):
    n_mp = MESH_MP
    rows, width = blocks[0].shape[0] // 2, blocks[0].shape[1]
    features = n_mp * width
    vmem = pl.BlockSpec(memory_space=pltpu.VMEM)
    hbm = pl.BlockSpec(memory_space=pltpu.HBM)
    return pl.pallas_call(
        functools.partial(encode_kernel, n_mp, slot, row),
        out_shape=[jax.ShapeDtypeStruct((rows, width), jnp.bfloat16)] * 8,
        in_specs=[pl.BlockSpec(memory_space=pltpu.SMEM)] + [vmem] * 3 + [hbm] * 11,
        out_specs=[vmem] * 8,
        scratch_shapes=[
            pltpu.VMEM((n_mp, rows, width), jnp.bfloat16),
            pltpu.VMEM((rows, features), jnp.bfloat16),
            pltpu.VMEM(w_qkv.shape, jnp.bfloat16),
            pltpu.VMEM(w_out.shape, jnp.bfloat16),
            pltpu.SemaphoreType.DMA((12,)),
        ],
        compiler_params=pltpu.CompilerParams(vmem_limit_bytes=VMEM_LIMIT),
        cost_estimate=pl.CostEstimate(
            flops=2 * rows * features * 4 * width,
            bytes_accessed=4 * rows * features,
            transcendentals=0,
        ),
    )(me, labels, gain, qk_gain, *blocks, w_qkv, w_out)


def pack_kernel(kept, labels_smem, labels_ref, patches_hbm, *refs):
    outs, sems = refs[:-1], refs[-1]
    pack_rows = labels_ref.shape[1]
    copies = []
    for k, out in enumerate(outs):
        rows = pl.ds((kept + k) * pack_rows, pack_rows)
        copies.append(
            pltpu.make_async_copy(patches_hbm.at[rows], out.at[pl.ds(0, pack_rows)], sems.at[k])
        )
        copies[-1].start()
    for k, out in enumerate(outs):
        tail = out.shape[0] - pack_rows
        tags = labels_ref[kept + k:kept + k + 1].astype(jnp.float32) + 1.0
        tags = jnp.broadcast_to(tags, (tail, pack_rows)).astype(jnp.bfloat16)
        out[pack_rows:, :pack_rows] = tags
        out[pack_rows:, pack_rows:] = jnp.zeros((tail, out.shape[1] - pack_rows), jnp.bfloat16)
        copies[k].wait()

        @pl.when(labels_smem[kept + k, 0] < 0)
        def _(out=out):
            out[:pack_rows] = jnp.zeros((pack_rows, out.shape[1]), jnp.bfloat16)


def pack_spare(labels, patches, kept, spare):
    pack_rows, width = labels.shape[1], patches.shape[1]
    vmem = pl.BlockSpec(memory_space=pltpu.VMEM)
    return pl.pallas_call(
        functools.partial(pack_kernel, kept),
        out_shape=[jax.ShapeDtypeStruct((pack_rows + 16, width), jnp.bfloat16)] * spare,
        in_specs=[pl.BlockSpec(memory_space=pltpu.SMEM), vmem, pl.BlockSpec(memory_space=pltpu.HBM)],
        out_specs=[vmem] * spare,
        scratch_shapes=[pltpu.SemaphoreType.DMA((spare,))],
        compiler_params=pltpu.CompilerParams(vmem_limit_bytes=SMALL_VMEM),
        cost_estimate=pl.CostEstimate(
            flops=0, bytes_accessed=4 * spare * pack_rows * width, transcendentals=0
        ),
    )(labels, labels, patches)


def merge_kernel(last, labels_smem, labels_ref, patches_hbm, a0, a1, a2, rows_ref, tags_ref, sems):
    pack_rows = labels_ref.shape[1]
    own = labels_smem[last, 0] >= 0
    head = pltpu.make_async_copy(
        patches_hbm.at[pl.ds(0, pack_rows)], rows_ref.at[pl.ds(0, pack_rows)], sems.at[0]
    )
    head.start()

    @pl.when(own)
    def _():
        source = patches_hbm.at[pl.ds(last * pack_rows, pack_rows)]
        copy = pltpu.make_async_copy(source, rows_ref.at[pl.ds(pack_rows, pack_rows)], sems.at[1])
        copy.start()
        copy.wait()
        tags_ref[...] = labels_ref[last:last + 1]

    @pl.when(jnp.logical_not(own))
    def _():
        rows_ref[pack_rows:] = a0[:pack_rows] + a1[:pack_rows] + a2[:pack_rows]
        tags = a0[pack_rows:, :pack_rows] + a1[pack_rows:, :pack_rows] + a2[pack_rows:, :pack_rows]
        tags_ref[...] = tags.astype(jnp.float32)[0:1].astype(jnp.int32) - 1

    head.wait()


def merge_last(labels, patches, arrived, last):
    pack_rows, width = labels.shape[1], patches.shape[1]
    vmem = pl.BlockSpec(memory_space=pltpu.VMEM)
    return pl.pallas_call(
        functools.partial(merge_kernel, last),
        out_shape=[
            jax.ShapeDtypeStruct((2 * pack_rows, width), jnp.bfloat16),
            jax.ShapeDtypeStruct((1, pack_rows), jnp.int32),
        ],
        in_specs=[pl.BlockSpec(memory_space=pltpu.SMEM), vmem, pl.BlockSpec(memory_space=pltpu.HBM)]
        + [vmem] * 3,
        out_specs=[vmem] * 2,
        scratch_shapes=[pltpu.SemaphoreType.DMA((2,))],
        compiler_params=pltpu.CompilerParams(vmem_limit_bytes=SMALL_VMEM),
        cost_estimate=pl.CostEstimate(
            flops=16_000_000_000, bytes_accessed=8 * pack_rows * width, transcendentals=0
        ),
    )(labels, labels, patches, *arrived)


def finish_kernel(labels_smem, x1, x2, xup, xdown, own, up, down, last, r1, r0, r2, out_hbm,
                  held, sems):
    rows = own.shape[0]
    terms = [[own, up, down]]
    for k, ref in enumerate((x1, x2)):
        cut = pl.ds(k * rows, rows)
        terms.append([ref, xup.at[cut], xdown.at[cut]])
    terms += [[last], [r0], [r1], [r2]]
    copies = []
    for pack, parts in enumerate(terms):
        values = sum(part[...].astype(jnp.float32) for part in parts)
        live = labels_smem[pack, 0] >= 0
        held[pack] = jnp.where(live, values, 0.0).astype(jnp.bfloat16)
        copies.append(
            pltpu.make_async_copy(
                held.at[pack], out_hbm.at[pl.ds(pack * rows, rows)], sems.at[pack]
            )
        )
        copies[-1].start()
    for copy in copies:
        copy.wait()


def finish(labels, *parts):
    home_packs, pack_rows = labels.shape
    width = parts[0].shape[1]
    vmem = pl.BlockSpec(memory_space=pltpu.VMEM)
    return pl.pallas_call(
        finish_kernel,
        out_shape=jax.ShapeDtypeStruct((home_packs * pack_rows, width), jnp.bfloat16),
        in_specs=[pl.BlockSpec(memory_space=pltpu.SMEM)] + [vmem] * len(parts),
        out_specs=pl.BlockSpec(memory_space=pl.ANY),
        scratch_shapes=[
            pltpu.VMEM((home_packs, pack_rows, width), jnp.bfloat16),
            pltpu.SemaphoreType.DMA((home_packs,)),
        ],
        compiler_params=pltpu.CompilerParams(vmem_limit_bytes=SMALL_VMEM),
        cost_estimate=pl.CostEstimate(
            flops=0, bytes_accessed=4 * home_packs * pack_rows * width, transcendentals=0
        ),
    )(labels, *parts)


class Order:
    def __init__(self, token):
        self.token = token

    def tie(self, *values):
        tied = lax.optimization_barrier(values + (self.token,))[:-1]
        return tied if len(tied) > 1 else tied[0]

    def mark(self, *values):
        self.token = lax.optimization_barrier((self.token,) + values)[0]


class Ring:
    def __init__(self, order):
        size = lax.axis_size("mp")
        self.order = order
        self.up = [(i, (i + 1) % size) for i in range(size)]
        self.down = [(i, (i - 1) % size) for i in range(size)]

    def send(self, rising, falling):
        rising, falling = self.order.tie(rising, falling)
        self.rising = lax.ppermute(rising, "mp", self.up)
        self.falling = lax.ppermute(falling, "mp", self.down)

    def done(self):
        self.order.mark(self.rising, self.falling)


class Gather(Ring):
    def __init__(self, order, block):
        super().__init__(order)
        self.half = block.shape[0] // 2
        self.blocks = [block]
        self.rising = self.falling = block

    def start(self):
        if len(self.blocks) < 7:
            self.send(self.rising, self.falling)
        else:
            self.send(self.rising[:self.half], self.falling[self.half:])

    def done(self):
        super().done()
        self.blocks += [self.rising, self.falling]


def add(first, second):
    return (first.astype(jnp.float32) + second.astype(jnp.float32)).astype(jnp.bfloat16)


def stack(parts):
    return jnp.concatenate(parts, axis=0) if len(parts) > 1 else parts[0]


class Scatter(Ring):
    def __init__(self, order, *packs):
        super().__init__(order)
        self.packs = packs
        self.step = 0

    def begin(self):
        self.send(self.packs[0][7], self.packs[1][7])

    def apart(self):
        chains = [Scatter(self.order, pack) for pack in self.packs]
        chains[0].rising, chains[0].falling = self.rising, None
        chains[1].rising, chains[1].falling = None, self.falling
        return chains

    def start(self):
        up, down = ([pack[5 - 2 * self.step + k] for pack in self.packs] for k in range(2))
        if len(self.packs) == 2 and self.step == 0:
            up[0], down[1] = add(up[0], self.rising), add(down[1], self.falling)
            self.send(stack(up), stack(down))
        else:
            rising, falling = stack(up), stack(down)
            self.send(
                rising if self.rising is None else add(rising, self.rising),
                falling if self.falling is None else add(falling, self.falling),
            )
        self.step += 1

    def terms(self):
        return self.packs[0][0], self.rising, self.falling


def total(ring):
    return sum(term.astype(jnp.float32) for term in ring.terms()).astype(jnp.bfloat16)


def local(patches, labels, ln_gain, w_qkv, qk_gain, w_out):
    groups = lax.axis_size("dp")
    home_packs, pack_rows = labels.shape
    spare = home_packs - WORK_P
    last = WORK_P - 1
    offsets = [1, groups // 2, groups - 1][:spare]
    me = lax.axis_index("mp").astype(jnp.int32).reshape(1)
    gain = ln_gain.reshape(1, -1)
    order = Order(labels[0, :1])

    def over_groups(values, sign, picks=(0, 1, 2)):
        return [
            lax.ppermute(
                value, "dp", [(i, (i + sign * offsets[pick]) % groups) for i in range(groups)]
            )
            for value, pick in zip(order.tie(*values), picks)
        ]

    def run(got, tags, row, slot):
        sums = encode(me, tags, row, gain, qk_gain, order.tie(*got.blocks), slot, w_qkv, w_out)
        order.mark(*sums)
        return sums

    def step(ring):
        ring.done()
        ring.start()

    x = Gather(order, patches[pack_rows:last * pack_rows])
    x.start()
    arrived = over_groups(pack_spare(labels, patches, WORK_P, spare), 1)
    step(x)
    order.mark(*arrived)
    rows, last_labels = merge_last(labels, patches, arrived, last)
    y = Gather(order, rows)
    y.start()
    step(x)
    y.done()
    step(x)
    x.done()
    y.start()
    sums1 = run(x, labels, 1, 0)
    step(y)
    sums2 = run(x, labels, 2, 1)
    rx = Scatter(order, sums1, sums2)
    step(y)
    rx.begin()
    y.done()
    step(rx)
    sums3 = run(y, last_labels, 0, 1)
    step(rx)
    sums0 = run(y, labels, 0, 0)
    rx.done()
    ry = Scatter(order, sums0, sums3)
    ry.begin()
    ry.done()
    r0, r3 = ry.apart()
    r3.start()
    r0.start()
    step(r3)
    step(r0)
    rx.start()
    step(r3)
    r3.done()
    sum3 = total(r3)
    returned = over_groups([sum3] * spare, -1, (1, 0, 2))
    step(r0)
    return finish(
        labels, sums1[0], sums2[0], rx.rising, rx.falling, *r0.terms(), sum3, *returned
    )


def solution(mesh):
    placed = (P("dp", "mp"), P("dp", None), P(), P(None, None, "mp"), P(None, "mp"), P("mp", None))
    return jax.shard_map(
        local, mesh=mesh, in_specs=placed, out_specs=P("dp", "mp"), check_vma=False
    )
```
